256 devices in a mesh: depth: 2 (over y_lo), freq: 128 (over z, x, y_hi, core).
Axes of the slice: x: 4, y: 4 (y_hi: 2, y_lo: 2; y = y_hi * 2 + y_lo), z: 8, core: 2. Of those that a mesh axis runs over, the one named last changes fastest.
Arguments:
- top_fields: bfloat16 [1, 256, 4, 256, 256], P(None, 'freq'), may hold values from -24 to 24
- slowness: float32 [2, 384, 384], P('depth'), may hold values from -5 to 5
- kernels: float32 [2, 256, 2, 81], P('depth', 'freq'), may hold values from -1 to 1
- offsets: int32 [1, 2], replicated, may hold values from 0 to 128
Outputs:
- image: float32 [2, 1, 8, 65536], P('depth', None, None, 'freq')
The draws below stay inside these ranges and needn't reach their ends.
All inputs are finite; a program needn't handle non-finite values.
Results may differ from the reference program's by a relative error of at most 0.0029.
Values may be sent and summed in bfloat16 or wider, within the bound.
A program may use at most 192 MiB of HBM per device.

```python
import math
import jax
import jax.numpy as jnp
from jax import lax

NX = 256
NY = 256
LAGS = 8
SLAB = 1
SHOTS = 1
MX = 384
MY = 384
FREQS = 256
DEPTHS = 2


def draw_kernels(key, part):
    key_phase = jax.random.fold_in(key, 11)
    key_taps = jax.random.fold_in(key, 12)
    phase_angle = jax.random.uniform(key_phase, (DEPTHS, FREQS, 1, 1), jnp.float32, -math.pi, math.pi)
    off_taps = jnp.clip(0.045 * jax.random.normal(key_taps, (DEPTHS, FREQS, 2, 81), jnp.float32), -0.2, 0.2)
    center_tap = 0.85 * jnp.concatenate((jnp.cos(phase_angle), jnp.sin(phase_angle)), axis=2)
    is_center = jnp.arange(81) == 40
    return jnp.where(is_center, center_tap, off_taps).astype(jnp.float32)


def spiked(values, key, source, target, parts, factor):
    def block_of(position):
        return (jnp.arange(values.shape[position]) // (values.shape[position] // parts)).reshape((-1,) + (1,) * (values.ndim - 1 - position))

    one_side = jax.random.permutation(key, parts)[block_of(target)]
    other_side = (block_of(target) + parts // 2) % parts
    return jnp.where((block_of(source) == one_side) | (block_of(source) == other_side), factor * values, values)


def steps_of(own_key, shape, pieces, least, top_value):
    gain, own = 1.0, jax.random.fold_in(own_key, 6)
    for axis_at, parts in pieces:
        draws = jnp.exp(jax.random.uniform(jax.random.fold_in(own, axis_at), (parts,), jnp.float32, least / len(pieces), top_value / len(pieces)))
        gain = gain * jnp.repeat(draws, shape[axis_at] // parts).reshape([-1 if axis == axis_at else 1 for axis in range(len(shape))])
    return gain


def noise(rng, extent, width, reach, pieces=(), held_as=jnp.bfloat16):
    array = jax.random.normal(rng, extent, jnp.float32) * width
    if len(pieces) > 0:
        array = steps_of(rng, extent, pieces, -0.22, 0.18) * array
    return jnp.clip(array, min=-reach, max=reach).astype(held_as)


def noise_with(key, shape, deviation, limit, shards, heavy, kind=jnp.bfloat16):
    entries = deviation * jax.random.normal(key, shape, jnp.float32)
    if shards:
        entries = entries * steps_of(key, shape, shards, -0.22, 0.18)
    return jnp.clip(spiked(entries, jax.random.fold_in(key, 3), *heavy), -limit, limit).astype(kind)


def setup_inputs(seed: int = 0) -> dict:
    splits = jax.random.split(jax.random.key(seed), 5)
    return {
        "top_fields": noise_with(splits[0], (SHOTS, FREQS, 4, NX, NY), 1.0, 24.0, ((1, 128),), (1, 3, 128, 5.5)),
        "slowness": noise(splits[1], (DEPTHS, MX, MY), 1.0, 5.0, ((0, 2),), jnp.float32),
        "kernels": draw_kernels(jax.random.fold_in(splits[4], 71), 0),
        "offsets": jax.random.randint(splits[3], (SHOTS, 2), 0, min(MX - NX, MY - NY) + 1).astype(jnp.int32),
    }


phase_gain = 3.0


def convolve(wavefield, kernel_taps):
    size_x = wavefield.shape[3]
    size_y = wavefield.shape[4]
    padded = jnp.pad(wavefield, ((0, 0), (0, 0), (0, 0), (4, 4), (4, 4)))
    real_part = padded[:, :, 0::2]
    imag_part = padded[:, :, 1::2]
    out_real = jnp.zeros(real_part.shape[:3] + (size_x, size_y), jnp.float32)
    out_imag = jnp.zeros(real_part.shape[:3] + (size_x, size_y), jnp.float32)
    for shift_x in range(9):
        for shift_y in range(9):
            tap_index = shift_x * 9 + shift_y
            tap_real = kernel_taps[:, 0, tap_index][None, :, None, None, None]
            tap_imag = kernel_taps[:, 1, tap_index][None, :, None, None, None]
            piece_real = real_part[:, :, :, shift_x:shift_x + size_x, shift_y:shift_y + size_y]
            piece_imag = imag_part[:, :, :, shift_x:shift_x + size_x, shift_y:shift_y + size_y]
            out_real = out_real + tap_real * piece_real - tap_imag * piece_imag
            out_imag = out_imag + tap_real * piece_imag + tap_imag * piece_real
    return out_real, out_imag


def extrapolate(wavefield, kernel_taps, screen_level, freq_weight):
    out_real, out_imag = convolve(wavefield, kernel_taps)
    angle_grid = phase_gain * freq_weight[None, :, None, None, None] * screen_level[:, None, None, :, :]
    cosine = jnp.cos(angle_grid)
    sine_grid = jnp.sin(angle_grid)
    new_real = out_real * cosine - out_imag * sine_grid
    new_imag = out_real * sine_grid + out_imag * cosine
    stacked = jnp.stack((new_real, new_imag), axis=3)
    return stacked.reshape(wavefield.shape)


def image_terms(wavefield, lag_count):
    half_lags = lag_count // 2
    size_x = wavefield.shape[3]
    padded = jnp.pad(wavefield, ((0, 0), (0, 0), (0, 0), (half_lags, half_lags), (0, 0)))
    collected = []
    for lag_index in range(lag_count):
        lag_shift = lag_index - half_lags
        source_part = padded[:, :, 0:2, half_lags - lag_shift:half_lags - lag_shift + size_x]
        receiver_part = padded[:, :, 2:4, half_lags + lag_shift:half_lags + lag_shift + size_x]
        collected.append(jnp.sum(source_part * receiver_part, axis=(1, 2)))
    return jnp.stack(collected, axis=1)


def screens_of(slowness, offsets, size_x, size_y):
    windows = []
    for shot_index in range(offsets.shape[0]):
        start_x = offsets[shot_index, 0].astype(jnp.int32)
        start_y = offsets[shot_index, 1].astype(jnp.int32)
        windows.append(lax.dynamic_slice(slowness, (jnp.zeros((), jnp.int32), start_x, start_y), (slowness.shape[0], size_x, size_y)))
    return jnp.stack(windows, axis=1)


def round_panel(wavefield):
    return lax.optimization_barrier(wavefield.astype(jnp.bfloat16)).astype(jnp.float32)


def freq_weights(first_freq, count_freqs, total_freqs):
    return (first_freq + jnp.arange(count_freqs, dtype=jnp.int32) + 1).astype(jnp.float32) / total_freqs


def reference(top_fields, slowness, kernels, offsets):
    screens = screens_of(slowness, offsets, NX, NY)

    def one_block(image_acc, first_freq):
        wavefield = lax.dynamic_slice_in_dim(top_fields, first_freq, 8, 1).astype(jnp.float32)
        kernel_block = lax.dynamic_slice_in_dim(kernels, first_freq, 8, 1)
        weights = freq_weights(first_freq, 8, FREQS)
        level_terms = []
        for depth_level in range(DEPTHS):
            wavefield = extrapolate(wavefield, kernel_block[depth_level], screens[depth_level], weights)
            level_terms.append(image_terms(wavefield, LAGS))
            if (depth_level + 1) % SLAB == 0 and depth_level < DEPTHS - 1:
                wavefield = round_panel(wavefield)
        return image_acc + jnp.stack(level_terms, axis=0), None

    initial = jnp.zeros((DEPTHS, SHOTS, LAGS, NX, NY), jnp.float32)
    starts = jnp.arange(FREQS // 8, dtype=jnp.int32) * 8
    image_acc, unused = lax.scan(one_block, initial, starts)
    return image_acc.reshape(DEPTHS, SHOTS, LAGS, NX * NY) * (float(FREQS) ** -0.5)
```

```python
import functools

import jax
import jax.numpy as jnp
from jax import lax
from jax.experimental import pallas as pl
from jax.experimental.pallas import tpu as pltpu
from jax.sharding import PartitionSpec as P

F32, BF16 = jnp.float32, jnp.bfloat16
MESH = pl.DeviceIdType.MESH

NZ, NXX = 8, 4


def iota(shape, dim):
    return lax.broadcasted_iota(jnp.int32, shape, dim)


def split_store(w_ref, rows, cols, value):
    high = value.astype(BF16)
    w_ref[0, rows, cols] = high
    w_ref[1, rows, cols] = (value - high.astype(F32)).astype(BF16)


def build_weights(taps_ref, w_ref, edge_ref):
    row, col = iota((128, 128), 0), iota((128, 128), 1)
    near = jnp.abs(col - row) <= 4
    row8, col8 = iota((8, 128), 0), iota((8, 128), 1)
    low = row8 < 4
    top_mask = col8 - row8 >= 124
    end_mask = col8 - (row8 + 120) <= -124
    edge_ref[...] = jnp.zeros_like(edge_ref)
    for a in range(9):
        circ = []
        for part in range(2):
            first = jnp.broadcast_to(taps_ref[part, a : a + 1, :], (128, 128))
            circ.append(pltpu.roll(first, 0, 1, stride=1, stride_axis=0))
        d_r, d_i = (jnp.where(near, m, 0.0) for m in circ)
        base = a * 256
        split_store(w_ref, pl.ds(base, 128), pl.ds(0, 128), d_r)
        split_store(w_ref, pl.ds(base, 128), pl.ds(128, 128), d_i)
        split_store(w_ref, pl.ds(base + 128, 128), pl.ds(0, 128), -d_i)
        split_store(w_ref, pl.ds(base + 128, 128), pl.ds(128, 128), d_r)
        t_r, t_i = (jnp.where(top_mask, m[0:8], 0.0) for m in circ)
        e_r, e_i = (jnp.where(end_mask, m[120:128], 0.0) for m in circ)
        rows = pl.ds(a * 8, 8)
        edge_ref[0, rows, 0:128] = jnp.where(low, t_r, -pltpu.roll(t_i, 4, 0))
        edge_ref[0, rows, 128:256] = jnp.where(low, t_i, pltpu.roll(t_r, 4, 0))
        edge_ref[1, rows, 0:128] = jnp.where(low, pltpu.roll(e_r, 4, 0), -e_i)
        edge_ref[1, rows, 128:256] = jnp.where(low, pltpu.roll(e_i, 4, 0), e_r)
    for side in range(2):
        split_store(w_ref, pl.ds(2304 + 128 * side, 128), pl.ds(0, 256), edge_ref[side])


def build_lhs(f_ref, g_ref, l_ref):
    lane = iota((264, 128), 1)
    for s in range(2):
        g_ref[s] = jnp.where(
            lane < 4, f_ref[2 + s, 0], jnp.where(lane < 8, pltpu.roll(f_ref[2 + s, 1], 4, 1), 0.0)
        )
        g_ref[2 + s] = jnp.where(
            lane < 4,
            pltpu.roll(f_ref[s, 0], 4, 1),
            jnp.where(lane < 8, pltpu.roll(f_ref[s, 1], 8, 1), 0.0),
        )
    for grp in range(4):

        @pl.loop(0, 8)
        def _(blk):
            row0 = pl.multiple_of(blk * 32, 32)
            out_rows = pl.ds(pl.multiple_of(grp * 256 + blk * 32, 32), 32)
            edge = jnp.zeros((32, 128), F32)
            for a in range(9):
                for part in range(2):
                    l_ref[out_rows, pl.ds(a * 256 + part * 128, 128)] = f_ref[
                        grp, part, pl.ds(row0 + a, 32), :
                    ].astype(BF16)
                piece = g_ref[grp, pl.ds(row0 + a, 32), :]
                edge = edge + (pltpu.roll(piece, 8 * a, 1) if a else piece)
            here = 2304 + 128 * (grp // 2)
            there = 2304 + 128 * (1 - grp // 2)
            l_ref[out_rows, pl.ds(here, 128)] = edge.astype(BF16)
            l_ref[out_rows, pl.ds(there, 128)] = jnp.zeros((32, 128), BF16)


def convolve(l_ref, w_ref, o_ref):
    @pl.loop(0, 2)
    def _(m):
        rows = pl.ds(pl.multiple_of(m * 512, 512), 512)
        left = l_ref[rows, :]
        o_ref[rows, :] = jnp.dot(left, w_ref[0], preferred_element_type=F32) + jnp.dot(
            left, w_ref[1], preferred_element_type=F32
        )


def apply_phase(o_ref, screen_ref, weight, f_ref):
    for yb in range(2):

        @pl.loop(0, 16)
        def _(blk):
            row0 = pl.multiple_of(blk * 16, 16)
            angle = (3.0 * weight) * screen_ref[pl.ds(row0, 16), pl.ds(yb * 128, 128)]
            cosine, sine = jnp.cos(angle), jnp.sin(angle)
            for s in range(2):
                grp = yb * 2 + s
                rows = pl.ds(pl.multiple_of(grp * 256 + row0, 16), 16)
                re = o_ref[rows, 0:128]
                im = o_ref[rows, 128:256]
                f_ref[grp, 0, pl.ds(row0 + 4, 16), :] = re * cosine - im * sine
                f_ref[grp, 1, pl.ds(row0 + 4, 16), :] = re * sine + im * cosine


def flip_source(f_ref, rev_ref):
    index = 7 - iota((8, 128), 0)
    for yb in range(2):
        for part in range(2):
            for t in range(33):
                rev_ref[yb, part, 8 * (32 - t) : 8 * (32 - t) + 8, :] = jnp.take_along_axis(
                    f_ref[yb * 2, part, 8 * t : 8 * t + 8, :], index, axis=0
                )


def image_piece(f_ref, rev_ref, img_ref, xx):
    for yb in range(2):

        @pl.loop(0, NZ)
        def _(z):
            blk = z * NXX + xx
            row0 = pl.multiple_of(blk * 8, 8)
            rev0 = pl.multiple_of(248 - blk * 8, 8)
            for j in range(8):
                s_rows = pl.ds(rev0 + (7 - j), 8)
                r_rows = pl.ds(row0 + j, 8)
                value = (
                    rev_ref[yb, 0, s_rows, :] * f_ref[yb * 2 + 1, 0, r_rows, :]
                    + rev_ref[yb, 1, s_rows, :] * f_ref[yb * 2 + 1, 1, r_rows, :]
                )
                to = pl.multiple_of(z * 64 + (j // 4) * 32 + (j % 2) * 16 + yb * 8, 8)
                img_ref[(j // 2) % 2, xx, pl.ds(to, 8), :] = value


def kernel(
    total,
    taps_ref, screen_ref, top_ref, out_ref,
    f_ref, g_ref, l_ref, w_ref, edge_ref, o_ref, rev_ref,
    taps_all, screens, img, rx1, tx2, rx2, acc2, rx3, acc3, rx4,
    local_sem, s0_send, s0_recv, s1_send, s1_recv, s2_send, s2_recv,
    s3_send, s3_recv, s4_send, s4_recv,
):
    d = lax.axis_index("depth")
    f = lax.axis_index("freq")
    core, yhi, xx, z = f % 2, (f // 2) % 2, (f // 4) % NXX, f // 16

    def device(depth=d, zc=z, xc=xx, yc=yhi, cc=core):
        return (depth, ((zc * NXX + xc) * 2 + yc) * 2 + cc)

    x_peers = [device(xc=(xx + off) % NXX) for off in range(1, NXX)]
    z_peers = [device(zc=(z + off) % NZ) for off in range(1, NZ)]
    core_peer = device(cc=1 - core)
    depth_peer = device(depth=1 - d)
    y_peers = [depth_peer, device(yc=1 - yhi), device(depth=1 - d, yc=1 - yhi)]
    everyone = [core_peer] + y_peers + x_peers + z_peers
    barrier = pltpu.get_barrier_semaphore()
    for peer in everyone:
        pl.semaphore_signal(barrier, inc=1, device_id=peer, device_id_type=MESH)

    own = [
        pltpu.make_async_copy(taps_ref.at[d], taps_all.at[d], local_sem.at[0]),
        pltpu.make_async_copy(screen_ref, screens.at[d], local_sem.at[1]),
    ]
    for copy in own:
        copy.start()

    f_ref[:, :, 0:8, :] = jnp.zeros((4, 2, 8, 128), F32)
    f_ref[:, :, 256:264, :] = jnp.zeros((4, 2, 8, 128), F32)
    for s in range(2):
        for part in range(2):
            for yb in range(2):
                f_ref[yb * 2 + s, part, 4:260, :] = top_ref[
                    d, 2 * s + part, :, yb * 128 : yb * 128 + 128
                ].astype(F32)

    pl.semaphore_wait(barrier, len(everyone))

    def remote(src, dst, send, recv, peer):
        return pltpu.make_async_remote_copy(
            src_ref=src, dst_ref=dst, send_sem=send, recv_sem=recv,
            device_id=peer, device_id_type=MESH,
        )

    swap_taps = remote(taps_ref.at[1 - d], taps_all.at[d], s0_send.at[0], s0_recv.at[0], depth_peer)
    swap_screen = remote(screen_ref, screens.at[d], s0_send.at[1], s0_recv.at[1], depth_peer)
    swap_taps.start()
    swap_screen.start()
    weight = (2 * f + d + 1).astype(F32) / total

    def stage1_copy(k, off):
        xp = (xx + off) % NXX
        return remote(
            img.at[k, 1 - core, xp], rx1.at[k, off], s1_send.at[k, off], s1_recv.at[k, off], core_peer
        )

    def stage2_copy(k, off):
        return remote(
            tx2.at[k, off - 1], rx2.at[k, off - 1],
            s2_send.at[k, off - 1], s2_recv.at[k, off - 1], x_peers[off - 1],
        )

    def stage3_copy(k, off):
        zp = (z + off) % NZ
        return remote(
            acc2.at[k, zp], rx3.at[k, off - 1],
            s3_send.at[k, off - 1], s3_recv.at[k, off - 1], z_peers[off - 1],
        )

    def stage4_keep(k):
        return remote(
            acc3.at[k, 1 - yhi], rx4.at[k, 0], s4_send.at[k, 0], s4_recv.at[k, 0], y_peers[1]
        )

    def stage4_give(k, yc):
        return remote(
            acc3.at[k, yc], rx4.at[k, 1 + yhi], s4_send.at[k, 1 + yc], s4_recv.at[k, 1 + yhi],
            device(depth=k, yc=yc),
        )

    def stage4_get(k, yc):
        return remote(
            acc3.at[k, 0], rx4.at[k, 1 + yc], s4_send.at[k, 0], s4_recv.at[k, 1 + yc], depth_peer
        )

    def make_image(k):
        flip_source(f_ref, rev_ref)
        for off in (1, 2, 3, 0):
            image_piece(f_ref, rev_ref, img.at[k], (xx + off) % NXX)
            stage1_copy(k, off).start()

    def after_core(k):
        for off in (1, 2, 3, 0):
            xp = (xx + off) % NXX
            stage1_copy(k, off).wait_recv()

            @pl.loop(0, 8)
            def _(part):
                rows = pl.ds(pl.multiple_of(part * 64, 64), 64)
                value = img[k, core, xp, rows, :] + rx1[k, off, rows, :]
                if off:
                    tx2[k, off - 1, rows, :] = value.astype(BF16)
                else:
                    acc2[k, part] = value

            if off:
                stage2_copy(k, off).start()

    def after_x(k):
        for off in range(1, NXX):
            stage2_copy(k, off).wait_recv()

        @pl.loop(0, NZ)
        def _(part):
            rows = pl.ds(pl.multiple_of(part * 64, 64), 64)
            value = acc2[k, part]
            for off in range(1, NXX):
                value = value + rx2[k, off - 1, rows, :].astype(F32)
            acc2[k, part] = value

        for off in range(1, NZ):
            stage3_copy(k, off).start()

    def after_z(k):
        for off in range(1, NZ):
            stage3_copy(k, off).wait_recv()
        value = acc2[k, z]
        for off in range(1, NZ):
            value = value + rx3[k, off - 1]
        acc3[k] = value.reshape(2, 32, 128)

        @pl.when(d == k)
        def _():
            stage4_keep(k).start()

        @pl.when(d != k)
        def _():
            for yc in range(2):
                stage4_give(k, yc).start()

    def after_y(k):
        @pl.when(d == k)
        def _():
            stage4_keep(k).wait_recv()
            for yc in range(2):
                stage4_get(k, yc).wait_recv()
            value = acc3[k, yhi] + rx4[k, 0] + rx4[k, 1] + rx4[k, 2]
            value = value * (total ** -0.5)
            for part in range(4):
                out_ref[:, part * 128 : part * 128 + 128] = value[part * 8 : part * 8 + 8]

    build_lhs(f_ref, g_ref, l_ref)
    own[0].wait()
    swap_taps.wait_recv()
    build_weights(taps_all.at[0], w_ref, edge_ref)
    convolve(l_ref, w_ref, o_ref)
    own[1].wait()
    swap_screen.wait_recv()
    apply_phase(o_ref, screens.at[0], weight, f_ref)
    make_image(0)
    build_lhs(f_ref, g_ref, l_ref)
    after_core(0)
    build_weights(taps_all.at[1], w_ref, edge_ref)
    convolve(l_ref, w_ref, o_ref)
    after_x(0)
    apply_phase(o_ref, screens.at[1], weight, f_ref)
    after_z(0)
    make_image(1)
    after_y(0)
    after_core(1)
    after_x(1)
    after_z(1)
    after_y(1)

    swap_taps.wait_send()
    swap_screen.wait_send()
    for k in range(2):
        for off in range(NXX):
            stage1_copy(k, off).wait_send()
        for off in range(1, NXX):
            stage2_copy(k, off).wait_send()
        for off in range(1, NZ):
            stage3_copy(k, off).wait_send()

        @pl.when(d == k)
        def _():
            stage4_keep(k).wait_send()

        @pl.when(d != k)
        def _():
            for yc in range(2):
                stage4_give(k, yc).wait_send()


def migrate(total, taps, screen, top):
    dma = pltpu.SemaphoreType.DMA
    vmem = pl.BlockSpec(memory_space=pltpu.VMEM)
    return pl.pallas_call(
        functools.partial(kernel, total),
        out_shape=jax.ShapeDtypeStruct((8, 512), F32),
        in_specs=[vmem] * 3,
        out_specs=vmem,
        scratch_shapes=[
            pltpu.VMEM((4, 2, 264, 128), F32),
            pltpu.VMEM((4, 264, 128), F32),
            pltpu.VMEM((1024, 2560), BF16),
            pltpu.VMEM((2, 2560, 256), BF16),
            pltpu.VMEM((2, 128, 256), F32),
            pltpu.VMEM((1024, 256), F32),
            pltpu.VMEM((2, 2, 264, 128), F32),
            pltpu.VMEM((2, 2, 16, 128), F32),
            pltpu.VMEM((2, 256, 256), F32),
            pltpu.VMEM((2, 2, NXX, 512, 128), F32),
            pltpu.VMEM((2, NXX, 512, 128), F32),
            pltpu.VMEM((2, 3, 512, 128), BF16),
            pltpu.VMEM((2, 3, 512, 128), BF16),
            pltpu.VMEM((2, NZ, 64, 128), F32),
            pltpu.VMEM((2, 7, 64, 128), F32),
            pltpu.VMEM((2, 2, 32, 128), F32),
            pltpu.VMEM((2, 3, 32, 128), F32),
            dma((2,)), dma((2,)), dma((2,)), dma((2, 4)), dma((2, 4)), dma((2, 3)), dma((2, 3)),
            dma((2, 7)), dma((2, 7)), dma((2, 3)), dma((2, 3)),
        ],
        compiler_params=pltpu.CompilerParams(
            collective_id=0, has_side_effects=True, vmem_limit_bytes=56 * 2**20
        ),
    )(taps, screen, top)


def arranged(kernels):
    taps = kernels.reshape(-1, 2, 9, 9)
    gap = jnp.zeros(taps.shape[:3] + (119,), F32)
    rows = jnp.concatenate((taps[..., 4::-1], gap, taps[..., :4:-1]), axis=-1)
    return jnp.pad(rows, ((0, 0), (0, 0), (0, 7), (0, 0)))


def local(total, top_fields, slowness, kernels, offsets):
    screen = lax.dynamic_slice(slowness[0], (offsets[0, 0], offsets[0, 1]), (256, 256))
    out = migrate(float(total), arranged(kernels[0]), screen, top_fields[0])
    return out[None, None]


def solution(mesh):
    return jax.shard_map(
        functools.partial(local, 256),
        mesh=mesh,
        in_specs=(
            P(None, "freq", None, None, None),
            P("depth", None, None),
            P("depth", "freq", None, None),
            P(),
        ),
        out_specs=P("depth", None, None, "freq"),
        check_vma=False,
    )
```

```python
import functools

import jax
import jax.numpy as jnp
from jax import lax
from jax.experimental import pallas as pl
from jax.experimental.pallas import tpu as pltpu
from jax.sharding import PartitionSpec as P

F32, BF16 = jnp.float32, jnp.bfloat16
MESH = pl.DeviceIdType.MESH

NZ, NXX = 8, 4


def iota(shape, dim):
    return lax.broadcasted_iota(jnp.int32, shape, dim)


def split_store(w_ref, rows, cols, value):
    high = value.astype(BF16)
    w_ref[0, rows, cols] = high
    w_ref[1, rows, cols] = (value - high.astype(F32)).astype(BF16)


def arrange_taps(taps_ref, pad_ref, out_ref):
    lane, row = iota((8, 128), 1), iota((8, 128), 0)
    used = (lane < 5) | (lane >= 124)
    place = jnp.where(lane < 5, 4 - lane, 132 - lane)
    pad_ref[...] = jnp.zeros_like(pad_ref)
    for fr in range(2):
        for part in range(2):
            pad_ref[2 * fr + part : 2 * fr + part + 1, 0:81] = taps_ref[fr, part : part + 1, :]
    for fr in range(2):
        for part in range(2):
            line = jnp.broadcast_to(pad_ref[2 * fr + part : 2 * fr + part + 1, :], (8, 128))
            for half in range(2):
                index = jnp.where(used, jnp.minimum(9 * (row + 8 * half), 72) + place, 127)
                out_ref[fr, part, 8 * half : 8 * half + 8, :] = jnp.take_along_axis(line, index, axis=1)


def build_weights(d, taps_ref, w_ref, edge_ref):
    row, col = iota((128, 128), 0), iota((128, 128), 1)
    near = jnp.abs(col - row) <= 4
    row8, col8 = iota((8, 128), 0), iota((8, 128), 1)
    low = row8 < 4
    top_mask = col8 - row8 >= 124
    end_mask = col8 - (row8 + 120) <= -124
    edge_ref[72:128, :] = jnp.zeros((56, 256), F32)
    for a in range(9):
        circ = []
        for part in range(2):
            first = jnp.broadcast_to(taps_ref[part, a : a + 1, :], (128, 128))
            circ.append(pltpu.roll(first, 0, 1, stride=1, stride_axis=0))
        d_r, d_i = (jnp.where(near, m, 0.0) for m in circ)
        base = a * 256
        split_store(w_ref, pl.ds(base, 128), pl.ds(0, 128), d_r)
        split_store(w_ref, pl.ds(base, 128), pl.ds(128, 128), d_i)
        split_store(w_ref, pl.ds(base + 128, 128), pl.ds(0, 128), -d_i)
        split_store(w_ref, pl.ds(base + 128, 128), pl.ds(128, 128), d_r)
        t_r, t_i = (jnp.where(top_mask, m[0:8], 0.0) for m in circ)
        e_r, e_i = (jnp.where(end_mask, m[120:128], 0.0) for m in circ)
        rows = pl.ds(a * 8, 8)
        edge_ref[rows, 0:128] = jnp.where(
            d == 0,
            jnp.where(low, t_r, -pltpu.roll(t_i, 4, 0)),
            jnp.where(low, pltpu.roll(e_r, 4, 0), -e_i),
        )
        edge_ref[rows, 128:256] = jnp.where(
            d == 0,
            jnp.where(low, t_i, pltpu.roll(t_r, 4, 0)),
            jnp.where(low, pltpu.roll(e_i, 4, 0), e_r),
        )
    split_store(w_ref, pl.ds(2304, 128), pl.ds(0, 256), edge_ref[...])


def build_lhs(f_ref, l_ref):
    for grp in range(4):

        @pl.loop(0, 8)
        def _(blk):
            row0 = pl.multiple_of(blk * 32, 32)
            out_rows = pl.ds(pl.multiple_of(grp * 256 + blk * 32, 32), 32)
            for a in range(9):
                for part in range(2):
                    l_ref[out_rows, pl.ds(a * 256 + part * 128, 128)] = f_ref[
                        grp, part, pl.ds(row0 + a, 32), :
                    ].astype(BF16)


def build_edge(g_ref, l_ref):
    for grp in range(4):

        @pl.loop(0, 8)
        def _(blk):
            row0 = pl.multiple_of(blk * 32, 32)
            out_rows = pl.ds(pl.multiple_of(grp * 256 + blk * 32, 32), 32)
            edge = g_ref[grp, pl.ds(row0, 32), :]
            for a in range(1, 9):
                edge = edge + pltpu.roll(g_ref[grp, pl.ds(row0 + a, 32), :], 8 * a, 1)
            l_ref[out_rows, pl.ds(2304, 128)] = edge.astype(BF16)


def pack_edge(d, f_ref, out_ref):
    lane = iota((256, 128), 1)
    packed = jnp.zeros((256, 128), F32)
    for grp in range(4):
        for part in range(2):
            first = 8 * grp + 4 * part
            turned = pltpu.roll(f_ref[grp, part, 4:260, :], 4 * (1 - d) + first, 1)
            packed = jnp.where((lane >= first) & (lane < first + 4), turned, packed)
    out_ref[...] = packed.astype(BF16)


def unpack_edge(in_ref, g_ref):
    lane = iota((256, 128), 1)
    packed = in_ref[...].astype(F32)
    for grp in range(4):
        turned = pltpu.roll(packed, 128 - 8 * grp, 1) if grp else packed
        g_ref[grp, 4:260, :] = jnp.where(lane < 8, turned, 0.0)


def top_edge(d, top_ref, g_ref):
    lane = iota((256, 128), 1)
    other = pl.ds(pl.multiple_of((1 - d) * 128, 128), 128)
    for fr in range(2):
        for s in range(2):
            re = pltpu.roll(top_ref[fr, 2 * s, :, other].astype(F32), 4 * d, 1)
            im = pltpu.roll(top_ref[fr, 2 * s + 1, :, other].astype(F32), 4 + 4 * d, 1)
            g_ref[2 * fr + s, 4:260, :] = jnp.where(lane < 4, re, jnp.where(lane < 8, im, 0.0))


def convolve(l_ref, w_ref, o_ref):
    @pl.loop(0, 2)
    def _(m):
        rows = pl.ds(pl.multiple_of(m * 512, 512), 512)
        left = l_ref[rows, :]
        o_ref[rows, :] = jnp.dot(left, w_ref[m, 0], preferred_element_type=F32) + jnp.dot(
            left, w_ref[m, 1], preferred_element_type=F32
        )


def apply_phase(o_ref, screen_ref, weights, f_ref):
    for fr in range(2):

        @pl.loop(0, 16)
        def _(blk):
            row0 = pl.multiple_of(blk * 16, 16)
            angle = (3.0 * weights[fr]) * screen_ref[pl.ds(row0, 16), :]
            cosine, sine = jnp.cos(angle), jnp.sin(angle)
            for s in range(2):
                grp = fr * 2 + s
                rows = pl.ds(pl.multiple_of(grp * 256 + row0, 16), 16)
                re = o_ref[rows, 0:128]
                im = o_ref[rows, 128:256]
                f_ref[grp, 0, pl.ds(row0 + 4, 16), :] = re * cosine - im * sine
                f_ref[grp, 1, pl.ds(row0 + 4, 16), :] = re * sine + im * cosine


def flip_source(f_ref, rev_ref):
    index = 7 - iota((8, 128), 0)
    for fr in range(2):
        for part in range(2):
            for t in range(33):
                rev_ref[fr, part, 8 * (32 - t) : 8 * (32 - t) + 8, :] = jnp.take_along_axis(
                    f_ref[fr * 2, part, 8 * t : 8 * t + 8, :], index, axis=0
                )


def image_piece(f_ref, rev_ref, img_ref, xx):
    @pl.loop(0, NZ)
    def _(z):
        blk = z * NXX + xx
        row0 = pl.multiple_of(blk * 8, 8)
        rev0 = pl.multiple_of(248 - blk * 8, 8)
        for j in range(8):
            s_rows = pl.ds(rev0 + (7 - j), 8)
            r_rows = pl.ds(row0 + j, 8)
            value = jnp.zeros((8, 128), F32)
            for fr in range(2):
                for part in range(2):
                    value = value + rev_ref[fr, part, s_rows, :] * f_ref[fr * 2 + 1, part, r_rows, :]
            to = pl.multiple_of(z * 32 + (j // 4) * 16 + (j % 2) * 8, 8)
            img_ref[(j // 2) % 2, xx, pl.ds(to, 8), :] = value


def kernel(
    total,
    taps_ref, screen_ref, top_ref, out_ref,
    f_ref, g_ref, l_ref, w_ref, edge_ref, o_ref, rev_ref, pad_ref,
    taps_all, screens, edge_tx, edge_rx, img, rx1, tx2, rx2, acc2, tx3, rx3, acc3, rx4,
    local_sem, s0_send, s0_recv, s1_send, s1_recv, s2_send, s2_recv,
    s3_send, s3_recv, s4_send, s4_recv,
):
    d = lax.axis_index("depth")
    f = lax.axis_index("freq")
    core, yhi, xx, z = f % 2, (f // 2) % 2, (f // 4) % NXX, f // 16

    def device(depth=d, zc=z, xc=xx, yc=yhi, cc=core):
        return (depth, ((zc * NXX + xc) * 2 + yc) * 2 + cc)

    x_peers = [device(xc=(xx + off) % NXX) for off in range(1, NXX)]
    z_peers = [device(zc=(z + off) % NZ) for off in range(1, NZ)]
    core_peer = device(cc=1 - core)
    depth_peer = device(depth=1 - d)
    y_peers = [depth_peer, device(yc=1 - yhi), device(depth=1 - d, yc=1 - yhi)]
    everyone = [core_peer] + y_peers + x_peers + z_peers
    barrier = pltpu.get_barrier_semaphore()
    for peer in everyone:
        pl.semaphore_signal(barrier, inc=1, device_id=peer, device_id_type=MESH)

    mine, theirs = (
        pl.ds(pl.multiple_of(half * 128, 128), 128) for half in (d, 1 - d)
    )
    own_screen = pltpu.make_async_copy(screen_ref.at[:, mine], screens.at[d], local_sem.at[0])
    own_screen.start()
    arrange_taps(taps_ref, pad_ref, taps_all.at[d])
    f_ref[:, :, 0:8, :] = jnp.zeros((4, 2, 8, 128), F32)
    f_ref[:, :, 256:264, :] = jnp.zeros((4, 2, 8, 128), F32)
    g_ref[:, 0:8, :] = jnp.zeros((4, 8, 128), F32)
    g_ref[:, 256:264, :] = jnp.zeros((4, 8, 128), F32)
    for fr in range(2):
        for s in range(2):
            for part in range(2):
                f_ref[fr * 2 + s, part, 4:260, :] = top_ref[fr, 2 * s + part, :, mine].astype(F32)
    top_edge(d, top_ref, g_ref)

    pl.semaphore_wait(barrier, len(everyone))

    def remote(src, dst, send, recv, peer):
        return pltpu.make_async_remote_copy(
            src_ref=src, dst_ref=dst, send_sem=send, recv_sem=recv,
            device_id=peer, device_id_type=MESH,
        )

    swap_taps = remote(taps_all.at[d], taps_all.at[d], s0_send.at[0], s0_recv.at[0], depth_peer)
    swap_screen = remote(
        screen_ref.at[:, theirs], screens.at[d], s0_send.at[1], s0_recv.at[1], depth_peer
    )
    swap_edge = remote(edge_tx, edge_rx, s0_send.at[2], s0_recv.at[2], depth_peer)
    swap_taps.start()
    swap_screen.start()
    weights = [(2 * f + fr + 1).astype(F32) / total for fr in range(2)]

    def stage1_copy(k, off):
        xp = (xx + off) % NXX
        return remote(
            img.at[k, 1 - core, xp], rx1.at[k, off], s1_send.at[k, off], s1_recv.at[k, off], core_peer
        )

    def stage2_copy(k, off):
        return remote(
            tx2.at[k, off - 1], rx2.at[k, off - 1],
            s2_send.at[k, off - 1], s2_recv.at[k, off - 1], x_peers[off - 1],
        )

    def stage3_copy(k, off):
        return remote(
            tx3.at[k, off - 1], rx3.at[k, off - 1],
            s3_send.at[k, off - 1], s3_recv.at[k, off - 1], z_peers[off - 1],
        )

    def stage4_keep(k):
        return remote(
            acc3.at[k, 1 - yhi], rx4.at[k, 0], s4_send.at[k, 0], s4_recv.at[k, 0], y_peers[1]
        )

    def stage4_give(k, yc):
        return remote(
            acc3.at[k, yc], rx4.at[k, 1 + yhi], s4_send.at[k, 1 + yc], s4_recv.at[k, 1 + yhi],
            device(depth=k, yc=yc),
        )

    def stage4_get(k, yc):
        return remote(
            acc3.at[k, 0], rx4.at[k, 1 + yc], s4_send.at[k, 0], s4_recv.at[k, 1 + yc], depth_peer
        )

    def make_image(k):
        flip_source(f_ref, rev_ref)
        for off in (1, 2, 3, 0):
            image_piece(f_ref, rev_ref, img.at[k], (xx + off) % NXX)
            stage1_copy(k, off).start()

    def after_core(k):
        for off in (1, 2, 3, 0):
            xp = (xx + off) % NXX
            stage1_copy(k, off).wait_recv()

            @pl.loop(0, 8)
            def _(part):
                rows = pl.ds(pl.multiple_of(part * 32, 32), 32)
                value = img[k, core, xp, rows, :] + rx1[k, off, rows, :]
                if off:
                    tx2[k, off - 1, rows, :] = value.astype(BF16)
                else:
                    acc2[k, part] = value

            if off:
                stage2_copy(k, off).start()

    def after_x(k):
        for off in range(1, NXX):
            stage2_copy(k, off).wait_recv()

        def total_of(part):
            rows = pl.ds(pl.multiple_of(part * 32, 32), 32)
            value = acc2[k, part]
            for off in range(1, NXX):
                value = value + rx2[k, off - 1, rows, :].astype(F32)
            return value

        for off in (4, 3, 5, 2, 6, 1, 7):
            tx3[k, off - 1] = total_of((z + off) % NZ).astype(BF16)
            stage3_copy(k, off).start()
        acc2[k, z] = total_of(z)

    def after_z(k):
        for off in range(1, NZ):
            stage3_copy(k, off).wait_recv()
        value = acc2[k, z]
        for off in range(1, NZ):
            value = value + rx3[k, off - 1].astype(F32)
        acc3[k] = value.reshape(2, 16, 128)

        @pl.when(d == k)
        def _():
            stage4_keep(k).start()

        @pl.when(d != k)
        def _():
            for yc in range(2):
                stage4_give(k, yc).start()

    def after_y(k):
        @pl.when(d == k)
        def _():
            stage4_keep(k).wait_recv()
            for yc in range(2):
                stage4_get(k, yc).wait_recv()
            scale = total ** -0.5
            near_half = (acc3[k, yhi] + rx4[k, 0]) * scale
            far_half = (rx4[k, 1] + rx4[k, 2]) * scale
            for low in range(2):
                rows = slice(low * 8, low * 8 + 8)
                out_ref[:, pl.ds(low * 256 + k * 128, 128)] = near_half[rows]
                out_ref[:, pl.ds(low * 256 + (1 - k) * 128, 128)] = far_half[rows]

    build_lhs(f_ref, l_ref)
    build_edge(g_ref, l_ref)
    swap_taps.wait_recv()
    for fr in range(2):
        build_weights(d, taps_all.at[0, fr], w_ref.at[fr], edge_ref)
    convolve(l_ref, w_ref, o_ref)
    own_screen.wait()
    swap_screen.wait_recv()
    apply_phase(o_ref, screens.at[0], weights, f_ref)
    pack_edge(d, f_ref, edge_tx)
    swap_edge.start()
    make_image(0)
    build_lhs(f_ref, l_ref)
    after_core(0)
    for fr in range(2):
        build_weights(d, taps_all.at[1, fr], w_ref.at[fr], edge_ref)
    swap_edge.wait_recv()
    unpack_edge(edge_rx, g_ref)
    build_edge(g_ref, l_ref)
    convolve(l_ref, w_ref, o_ref)
    apply_phase(o_ref, screens.at[1], weights, f_ref)
    after_x(0)
    make_image(1)
    after_core(1)
    after_z(0)
    after_x(1)
    after_y(0)
    after_z(1)
    after_y(1)

    swap_edge.wait_send()
    swap_taps.wait_send()
    swap_screen.wait_send()
    for k in range(2):
        for off in range(NXX):
            stage1_copy(k, off).wait_send()
        for off in range(1, NXX):
            stage2_copy(k, off).wait_send()
        for off in range(1, NZ):
            stage3_copy(k, off).wait_send()

        @pl.when(d == k)
        def _():
            stage4_keep(k).wait_send()

        @pl.when(d != k)
        def _():
            for yc in range(2):
                stage4_give(k, yc).wait_send()


def migrate(total, taps, screen, top):
    dma = pltpu.SemaphoreType.DMA
    vmem = pl.BlockSpec(memory_space=pltpu.VMEM)
    return pl.pallas_call(
        functools.partial(kernel, total),
        out_shape=jax.ShapeDtypeStruct((8, 512), F32),
        in_specs=[vmem] * 3,
        out_specs=vmem,
        scratch_shapes=[
            pltpu.VMEM((4, 2, 264, 128), F32),
            pltpu.VMEM((4, 264, 128), F32),
            pltpu.VMEM((1024, 2432), BF16),
            pltpu.VMEM((2, 2, 2432, 256), BF16),
            pltpu.VMEM((128, 256), F32),
            pltpu.VMEM((1024, 256), F32),
            pltpu.VMEM((2, 2, 264, 128), F32),
            pltpu.VMEM((8, 128), F32),
            pltpu.VMEM((2, 2, 2, 16, 128), F32),
            pltpu.VMEM((2, 256, 128), F32),
            pltpu.VMEM((256, 128), BF16),
            pltpu.VMEM((256, 128), BF16),
            pltpu.VMEM((2, 2, NXX, 256, 128), F32),
            pltpu.VMEM((2, NXX, 256, 128), F32),
            pltpu.VMEM((2, 3, 256, 128), BF16),
            pltpu.VMEM((2, 3, 256, 128), BF16),
            pltpu.VMEM((2, NZ, 32, 128), F32),
            pltpu.VMEM((2, 7, 32, 128), BF16),
            pltpu.VMEM((2, 7, 32, 128), BF16),
            pltpu.VMEM((2, 2, 16, 128), F32),
            pltpu.VMEM((2, 3, 16, 128), F32),
            dma((1,)), dma((3,)), dma((3,)), dma((2, 4)), dma((2, 4)), dma((2, 3)), dma((2, 3)),
            dma((2, 7)), dma((2, 7)), dma((2, 3)), dma((2, 3)),
        ],
        compiler_params=pltpu.CompilerParams(
            collective_id=0, has_side_effects=True, vmem_limit_bytes=56 * 2**20
        ),
    )(taps, screen, top)


def local(total, top_fields, slowness, kernels, offsets):
    screen = lax.dynamic_slice(slowness[0], (offsets[0, 0], offsets[0, 1]), (256, 256))
    out = migrate(float(total), kernels[0], screen, top_fields[0])
    return out[None, None]


def solution(mesh):
    return jax.shard_map(
        functools.partial(local, 256),
        mesh=mesh,
        in_specs=(
            P(None, "freq", None, None, None),
            P("depth", None, None),
            P("depth", "freq", None, None),
            P(),
        ),
        out_specs=P("depth", None, None, "freq"),
        check_vma=False,
    )
```

```python
import functools

import jax
import jax.numpy as jnp
from jax import lax
from jax.experimental import pallas as pl
from jax.experimental.pallas import tpu as pltpu
from jax.sharding import PartitionSpec as P

F32, BF16 = jnp.float32, jnp.bfloat16
MESH = pl.DeviceIdType.MESH

NZ, NXX = 8, 4


def iota(shape, dim):
    return lax.broadcasted_iota(jnp.int32, shape, dim)


def split_store(w_ref, rows, cols, value):
    high = value.astype(BF16)
    w_ref[0, rows, cols] = high
    w_ref[1, rows, cols] = (value - high.astype(F32)).astype(BF16)


def arrange_taps(taps_ref, pad_ref, out_ref):
    lane, row = iota((8, 128), 1), iota((8, 128), 0)
    used = (lane < 5) | (lane >= 124)
    place = jnp.where(lane < 5, 4 - lane, 132 - lane)
    pad_ref[...] = jnp.zeros_like(pad_ref)
    for fr in range(2):
        for part in range(2):
            pad_ref[2 * fr + part : 2 * fr + part + 1, 0:81] = taps_ref[fr, part : part + 1, :]
    for fr in range(2):
        for part in range(2):
            line = jnp.broadcast_to(pad_ref[2 * fr + part : 2 * fr + part + 1, :], (8, 128))
            for half in range(2):
                index = jnp.where(used, jnp.minimum(9 * (row + 8 * half), 72) + place, 127)
                out_ref[fr, part, 8 * half : 8 * half + 8, :] = jnp.take_along_axis(line, index, axis=1)


def build_weights(d, taps_ref, w_ref, edge_ref):
    row, col = iota((128, 128), 0), iota((128, 128), 1)
    near = jnp.abs(col - row) <= 4
    row8, col8 = iota((8, 128), 0), iota((8, 128), 1)
    low = row8 < 4
    top_mask = col8 - row8 >= 124
    end_mask = col8 - (row8 + 120) <= -124
    edge_ref[72:128, :] = jnp.zeros((56, 256), F32)
    for a in range(9):
        circ = []
        for part in range(2):
            first = jnp.broadcast_to(taps_ref[part, a : a + 1, :], (128, 128))
            circ.append(pltpu.roll(first, 0, 1, stride=1, stride_axis=0))
        d_r, d_i = (jnp.where(near, m, 0.0) for m in circ)
        base = a * 256
        split_store(w_ref, pl.ds(base, 128), pl.ds(0, 128), d_r)
        split_store(w_ref, pl.ds(base, 128), pl.ds(128, 128), d_i)
        split_store(w_ref, pl.ds(base + 128, 128), pl.ds(0, 128), -d_i)
        split_store(w_ref, pl.ds(base + 128, 128), pl.ds(128, 128), d_r)
        t_r, t_i = (jnp.where(top_mask, m[0:8], 0.0) for m in circ)
        e_r, e_i = (jnp.where(end_mask, m[120:128], 0.0) for m in circ)
        rows = pl.ds(a * 8, 8)
        edge_ref[rows, 0:128] = jnp.where(
            d == 0,
            jnp.where(low, t_r, -pltpu.roll(t_i, 4, 0)),
            jnp.where(low, pltpu.roll(e_r, 4, 0), -e_i),
        )
        edge_ref[rows, 128:256] = jnp.where(
            d == 0,
            jnp.where(low, t_i, pltpu.roll(t_r, 4, 0)),
            jnp.where(low, pltpu.roll(e_i, 4, 0), e_r),
        )
    split_store(w_ref, pl.ds(2304, 128), pl.ds(0, 256), edge_ref[...])


def pack_edge(d, f_ref, out_ref):
    lane = iota((256, 128), 1)
    packed = jnp.zeros((256, 128), F32)
    for grp in range(4):
        for part in range(2):
            first = 8 * grp + 4 * part
            turned = pltpu.roll(f_ref[grp, part, 4:260, :], 4 * (1 - d) + first, 1)
            packed = jnp.where((lane >= first) & (lane < first + 4), turned, packed)
    out_ref[...] = packed.astype(BF16)


def unpack_edge(in_ref, g_ref):
    lane = iota((256, 128), 1)
    packed = in_ref[...].astype(F32)
    for grp in range(4):
        turned = pltpu.roll(packed, 128 - 8 * grp, 1) if grp else packed
        g_ref[grp, 4:260, :] = jnp.where(lane < 8, turned, 0.0)


def top_edge(d, top_ref, g_ref):
    lane = iota((256, 128), 1)
    other = pl.ds(pl.multiple_of((1 - d) * 128, 128), 128)
    for fr in range(2):
        for s in range(2):
            re = pltpu.roll(top_ref[fr, 2 * s, :, other].astype(F32), 4 * d, 1)
            im = pltpu.roll(top_ref[fr, 2 * s + 1, :, other].astype(F32), 4 + 4 * d, 1)
            g_ref[2 * fr + s, 4:260, :] = jnp.where(lane < 4, re, jnp.where(lane < 8, im, 0.0))


def convolve(f_ref, g_ref, w_ref, o_ref):
    for fr in range(2):
        fields = []
        for grp in (2 * fr, 2 * fr + 1):
            pieces = [
                f_ref[grp, part, pl.ds(a, 256), :].astype(BF16) for a in range(9) for part in range(2)
            ]
            edge = g_ref[grp, pl.ds(0, 256), :]
            for a in range(1, 9):
                edge = edge + pltpu.roll(g_ref[grp, pl.ds(a, 256), :], 8 * a, 1)
            pieces.append(edge.astype(BF16))
            fields.append(jnp.concatenate(pieces, axis=1))
        left = jnp.concatenate(fields, axis=0)
        o_ref[fr * 512 : fr * 512 + 512, :] = jnp.dot(
            left, w_ref[fr, 0], preferred_element_type=F32
        ) + jnp.dot(left, w_ref[fr, 1], preferred_element_type=F32)


def cos_sin(angle):
    turns = jnp.round(angle * 0.6366197723675814)
    y = ((angle - turns * 1.5703125) - turns * 4.837512969970703e-4) - turns * 7.549789948768648e-8
    z = y * y
    sine = y + y * z * (-1.6666654611e-1 + z * (8.3321608736e-3 + z * -1.9515295891e-4))
    cosine = (1.0 - 0.5 * z) + z * z * (
        4.166664568298827e-2 + z * (-1.388731625493765e-3 + z * 2.443315711809948e-5)
    )
    quarter = turns.astype(jnp.int32)
    odd = (quarter & 1) == 1
    out_sine = jnp.where(odd, cosine, sine)
    out_cosine = jnp.where(odd, sine, cosine)
    return (
        jnp.where(((quarter + 1) & 2) == 2, -out_cosine, out_cosine),
        jnp.where((quarter & 2) == 2, -out_sine, out_sine),
    )


def cut_screen(slow_ref, off_x, off_y, half, wide_ref, out_ref):
    lane = iota((32, 128), 1)
    start = jnp.zeros((32, 128), jnp.int32) + (off_y + 128 * half)

    @pl.loop(0, 12)
    def _(blk):
        rows = pl.ds(pl.multiple_of(blk * 32, 32), 32)
        value = jnp.where(
            lane >= start,
            slow_ref[rows, 0:128],
            jnp.where(lane + 128 >= start, slow_ref[rows, 128:256], slow_ref[rows, 256:384]),
        )
        for bit in range(7):
            turned = pltpu.roll(value, 128 - (1 << bit), 1)
            value = jnp.where((start & (1 << bit)) > 0, turned, value)
        wide_ref[rows, :] = value

    @pl.loop(0, 8)
    def _(blk):
        row0 = pl.multiple_of(blk * 32, 32)
        out_ref[pl.ds(row0, 32), :] = wide_ref[pl.ds(off_x + row0, 32), :]


def apply_phase(o_ref, screen_ref, weights, f_ref):
    for fr in range(2):

        @pl.loop(0, 16)
        def _(blk):
            row0 = pl.multiple_of(blk * 16, 16)
            angle = (3.0 * weights[fr]) * screen_ref[pl.ds(row0, 16), :]
            cosine, sine = cos_sin(angle)
            for s in range(2):
                grp = fr * 2 + s
                rows = pl.ds(pl.multiple_of(grp * 256 + row0, 16), 16)
                re = o_ref[rows, 0:128]
                im = o_ref[rows, 128:256]
                f_ref[grp, 0, pl.ds(row0 + 4, 16), :] = re * cosine - im * sine
                f_ref[grp, 1, pl.ds(row0 + 4, 16), :] = re * sine + im * cosine


def flip_source(f_ref, rev_ref):
    index = 7 - iota((8, 128), 0)
    for fr in range(2):
        for part in range(2):
            for t in range(33):
                rev_ref[fr, part, 8 * (32 - t) : 8 * (32 - t) + 8, :] = jnp.take_along_axis(
                    f_ref[fr * 2, part, 8 * t : 8 * t + 8, :], index, axis=0
                )


def image_piece(f_ref, rev_ref, img_ref, xx):
    @pl.loop(0, NZ)
    def _(z):
        blk = z * NXX + xx
        row0 = pl.multiple_of(blk * 8, 8)
        rev0 = pl.multiple_of(248 - blk * 8, 8)
        for j in range(8):
            s_rows = pl.ds(rev0 + (7 - j), 8)
            r_rows = pl.ds(row0 + j, 8)
            value = jnp.zeros((8, 128), F32)
            for fr in range(2):
                for part in range(2):
                    value = value + rev_ref[fr, part, s_rows, :] * f_ref[fr * 2 + 1, part, r_rows, :]
            to = pl.multiple_of(z * 32 + (j // 4) * 16 + (j % 2) * 8, 8)
            img_ref[(j // 2) % 2, xx, pl.ds(to, 8), :] = value


def kernel(
    total,
    offsets_ref, taps_ref, slow_ref, top_ref, out_ref,
    f_ref, g_ref, w_ref, edge_ref, o_ref, rev_ref, pad_ref,
    wide_ref, taps_all, screens, screen_tx, edge_tx, edge_rx, img, rx1, tx2, rx2, acc2, tx3, rx3, acc3, rx4,
    s0_send, s0_recv, s1_send, s1_recv, s2_send, s2_recv,
    s3_send, s3_recv, s4_send, s4_recv,
):
    d = lax.axis_index("depth")
    f = lax.axis_index("freq")
    core, yhi, xx, z = f % 2, (f // 2) % 2, (f // 4) % NXX, f // 16

    def device(depth=d, zc=z, xc=xx, yc=yhi, cc=core):
        return (depth, ((zc * NXX + xc) * 2 + yc) * 2 + cc)

    x_peers = [device(xc=(xx + off) % NXX) for off in range(1, NXX)]
    z_peers = [device(zc=(z + off) % NZ) for off in range(1, NZ)]
    core_peer = device(cc=1 - core)
    depth_peer = device(depth=1 - d)
    y_peers = [depth_peer, device(yc=1 - yhi), device(depth=1 - d, yc=1 - yhi)]
    everyone = [core_peer] + y_peers + x_peers + z_peers
    barrier = pltpu.get_barrier_semaphore()
    for peer in everyone:
        pl.semaphore_signal(barrier, inc=1, device_id=peer, device_id_type=MESH)

    mine = pl.ds(pl.multiple_of(d * 128, 128), 128)
    arrange_taps(taps_ref, pad_ref, taps_all.at[d])
    f_ref[:, :, 0:8, :] = jnp.zeros((4, 2, 8, 128), F32)
    f_ref[:, :, 256:264, :] = jnp.zeros((4, 2, 8, 128), F32)
    g_ref[:, 0:8, :] = jnp.zeros((4, 8, 128), F32)
    g_ref[:, 256:264, :] = jnp.zeros((4, 8, 128), F32)
    for fr in range(2):
        for s in range(2):
            for part in range(2):
                f_ref[fr * 2 + s, part, 4:260, :] = top_ref[fr, 2 * s + part, :, mine].astype(F32)
    top_edge(d, top_ref, g_ref)
    off_x, off_y = offsets_ref[0, 0], offsets_ref[0, 1]
    cut_screen(slow_ref, off_x, off_y, 1 - d, wide_ref, screen_tx)
    cut_screen(slow_ref, off_x, off_y, d, wide_ref, screens.at[d])
    for fr in range(2):
        build_weights(d, taps_all.at[d, fr], w_ref.at[d, fr], edge_ref)

    pl.semaphore_wait(barrier, len(everyone))

    def remote(src, dst, send, recv, peer):
        return pltpu.make_async_remote_copy(
            src_ref=src, dst_ref=dst, send_sem=send, recv_sem=recv,
            device_id=peer, device_id_type=MESH,
        )

    swap_taps = remote(taps_all.at[d], taps_all.at[d], s0_send.at[0], s0_recv.at[0], depth_peer)
    swap_screen = remote(
        screen_tx, screens.at[d], s0_send.at[1], s0_recv.at[1], depth_peer
    )
    swap_edge = remote(edge_tx, edge_rx, s0_send.at[2], s0_recv.at[2], depth_peer)
    swap_taps.start()
    swap_screen.start()
    weights = [(2 * f + fr + 1).astype(F32) / total for fr in range(2)]

    def stage1_copy(k, off):
        xp = (xx + off) % NXX
        return remote(
            img.at[k, 1 - core, xp], rx1.at[k, off], s1_send.at[k, off], s1_recv.at[k, off], core_peer
        )

    def stage2_copy(k, off):
        return remote(
            tx2.at[k, off - 1], rx2.at[k, off - 1],
            s2_send.at[k, off - 1], s2_recv.at[k, off - 1], x_peers[off - 1],
        )

    def stage3_copy(k, off):
        return remote(
            tx3.at[k, off - 1], rx3.at[k, off - 1],
            s3_send.at[k, off - 1], s3_recv.at[k, off - 1], z_peers[off - 1],
        )

    def stage4_keep(k):
        return remote(
            acc3.at[k, 1 - yhi], rx4.at[k, 0], s4_send.at[k, 0], s4_recv.at[k, 0], y_peers[1]
        )

    def stage4_give(k, yc):
        return remote(
            acc3.at[k, yc], rx4.at[k, 1 + yhi], s4_send.at[k, 1 + yc], s4_recv.at[k, 1 + yhi],
            device(depth=k, yc=yc),
        )

    def stage4_get(k, yc):
        return remote(
            acc3.at[k, 0], rx4.at[k, 1 + yc], s4_send.at[k, 0], s4_recv.at[k, 1 + yc], depth_peer
        )

    def make_image(k):
        flip_source(f_ref, rev_ref)
        for off in (1, 2, 3, 0):
            image_piece(f_ref, rev_ref, img.at[k], (xx + off) % NXX)
            stage1_copy(k, off).start()

    def after_core(k):
        for off in (1, 2, 3, 0):
            xp = (xx + off) % NXX
            stage1_copy(k, off).wait_recv()

            @pl.loop(0, 8)
            def _(part):
                rows = pl.ds(pl.multiple_of(part * 32, 32), 32)
                value = img[k, core, xp, rows, :] + rx1[k, off, rows, :]
                if off:
                    tx2[k, off - 1, rows, :] = value.astype(BF16)
                else:
                    acc2[k, part] = value

            if off:
                stage2_copy(k, off).start()

    def after_x(k):
        for off in range(1, NXX):
            stage2_copy(k, off).wait_recv()

        def total_of(part):
            rows = pl.ds(pl.multiple_of(part * 32, 32), 32)
            value = acc2[k, part]
            for off in range(1, NXX):
                value = value + rx2[k, off - 1, rows, :].astype(F32)
            return value

        for off in (4, 3, 5, 2, 6, 1, 7):
            tx3[k, off - 1] = total_of((z + off) % NZ).astype(BF16)
            stage3_copy(k, off).start()
        acc2[k, z] = total_of(z)

    def after_z(k):
        for off in range(1, NZ):
            stage3_copy(k, off).wait_recv()
        value = acc2[k, z]
        for off in range(1, NZ):
            value = value + rx3[k, off - 1].astype(F32)
        acc3[k] = value.reshape(2, 16, 128)

        @pl.when(d == k)
        def _():
            stage4_keep(k).start()

        @pl.when(d != k)
        def _():
            for yc in range(2):
                stage4_give(k, yc).start()

    def after_y(k):
        @pl.when(d == k)
        def _():
            stage4_keep(k).wait_recv()
            for yc in range(2):
                stage4_get(k, yc).wait_recv()
            near_half = acc3[k, yhi] + rx4[k, 0]
            far_half = rx4[k, 1] + rx4[k, 2]
            for low in range(2):
                rows = slice(low * 8, low * 8 + 8)
                out_ref[:, pl.ds(low * 256 + k * 128, 128)] = near_half[rows]
                out_ref[:, pl.ds(low * 256 + (1 - k) * 128, 128)] = far_half[rows]

    swap_taps.wait_recv()
    for fr in range(2):
        build_weights(d, taps_all.at[1 - d, fr], w_ref.at[1 - d, fr], edge_ref)
    convolve(f_ref, g_ref, w_ref.at[0], o_ref)
    swap_screen.wait_recv()
    apply_phase(o_ref, screens.at[0], weights, f_ref)
    pack_edge(d, f_ref, edge_tx)
    swap_edge.start()
    make_image(0)
    swap_edge.wait_recv()
    unpack_edge(edge_rx, g_ref)
    after_core(0)
    convolve(f_ref, g_ref, w_ref.at[1], o_ref)
    apply_phase(o_ref, screens.at[1], weights, f_ref)
    make_image(1)
    after_x(0)
    after_core(1)
    after_z(0)
    after_x(1)
    after_y(0)
    after_z(1)
    after_y(1)

    swap_edge.wait_send()
    swap_taps.wait_send()
    swap_screen.wait_send()
    for k in range(2):
        for off in range(NXX):
            stage1_copy(k, off).wait_send()
        for off in range(1, NXX):
            stage2_copy(k, off).wait_send()
        for off in range(1, NZ):
            stage3_copy(k, off).wait_send()

        @pl.when(d == k)
        def _():
            stage4_keep(k).wait_send()

        @pl.when(d != k)
        def _():
            for yc in range(2):
                stage4_give(k, yc).wait_send()


def migrate(total, offsets, taps, slowness, top):
    dma = pltpu.SemaphoreType.DMA
    vmem = pl.BlockSpec(memory_space=pltpu.VMEM)
    return pl.pallas_call(
        functools.partial(kernel, total),
        out_shape=jax.ShapeDtypeStruct((8, 512), F32),
        in_specs=[pl.BlockSpec(memory_space=pltpu.SMEM)] + [vmem] * 3,
        out_specs=vmem,
        scratch_shapes=[
            pltpu.VMEM((4, 2, 264, 128), F32),
            pltpu.VMEM((4, 264, 128), F32),
            pltpu.VMEM((2, 2, 2, 2432, 256), BF16),
            pltpu.VMEM((128, 256), F32),
            pltpu.VMEM((1024, 256), F32),
            pltpu.VMEM((2, 2, 264, 128), F32),
            pltpu.VMEM((8, 128), F32),
            pltpu.VMEM((384, 128), F32),
            pltpu.VMEM((2, 2, 2, 16, 128), F32),
            pltpu.VMEM((2, 256, 128), F32),
            pltpu.VMEM((256, 128), F32),
            pltpu.VMEM((256, 128), BF16),
            pltpu.VMEM((256, 128), BF16),
            pltpu.VMEM((2, 2, NXX, 256, 128), F32),
            pltpu.VMEM((2, NXX, 256, 128), F32),
            pltpu.VMEM((2, 3, 256, 128), BF16),
            pltpu.VMEM((2, 3, 256, 128), BF16),
            pltpu.VMEM((2, NZ, 32, 128), F32),
            pltpu.VMEM((2, 7, 32, 128), BF16),
            pltpu.VMEM((2, 7, 32, 128), BF16),
            pltpu.VMEM((2, 2, 16, 128), F32),
            pltpu.VMEM((2, 3, 16, 128), F32),
            dma((3,)), dma((3,)), dma((2, 4)), dma((2, 4)), dma((2, 3)), dma((2, 3)),
            dma((2, 7)), dma((2, 7)), dma((2, 3)), dma((2, 3)),
        ],
        compiler_params=pltpu.CompilerParams(
            collective_id=0, has_side_effects=True, vmem_limit_bytes=56 * 2**20
        ),
    )(offsets, taps, slowness, top)


def local(total, top_fields, slowness, kernels, offsets):
    out = migrate(float(total), offsets, kernels[0], slowness[0], top_fields[0])
    return out[None, None] * float(total) ** -0.5


def solution(mesh):
    return jax.shard_map(
        functools.partial(local, 256),
        mesh=mesh,
        in_specs=(
            P(None, "freq", None, None, None),
            P("depth", None, None),
            P("depth", "freq", None, None),
            P(),
        ),
        out_specs=P("depth", None, None, "freq"),
        check_vma=False,
    )
```

```python
import functools

import jax
import jax.numpy as jnp
from jax import lax
from jax.experimental import pallas as pl
from jax.experimental.pallas import tpu as pltpu
from jax.sharding import PartitionSpec as P

F32, BF16 = jnp.float32, jnp.bfloat16
MESH = pl.DeviceIdType.MESH

NZ, NXX = 8, 4
X_ORDER = (2, 1, 3, 0)


def iota(shape, dim):
    return lax.broadcasted_iota(jnp.int32, shape, dim)


def split_store(w_ref, rows, cols, value):
    high = value.astype(BF16)
    w_ref[0, rows, cols] = high
    w_ref[1, rows, cols] = (value - high.astype(F32)).astype(BF16)


def arrange_taps(taps_ref, pad_ref, out_ref):
    lane, row = iota((8, 128), 1), iota((8, 128), 0)
    used = (lane < 5) | (lane >= 124)
    place = jnp.where(lane < 5, 4 - lane, 132 - lane)
    pad_ref[...] = jnp.zeros_like(pad_ref)
    for fr in range(2):
        for part in range(2):
            pad_ref[2 * fr + part : 2 * fr + part + 1, 0:81] = taps_ref[fr, part : part + 1, :]
    for fr in range(2):
        for part in range(2):
            line = jnp.broadcast_to(pad_ref[2 * fr + part : 2 * fr + part + 1, :], (8, 128))
            for half in range(2):
                index = jnp.where(used, jnp.minimum(9 * (row + 8 * half), 72) + place, 127)
                out_ref[fr, part, 8 * half : 8 * half + 8, :] = jnp.take_along_axis(line, index, axis=1)


def build_weights(d, taps_ref, w_ref, edge_ref):
    row, col = iota((128, 128), 0), iota((128, 128), 1)
    near = jnp.abs(col - row) <= 4
    row8, col8 = iota((8, 128), 0), iota((8, 128), 1)
    low = row8 < 4
    top_mask = col8 - row8 >= 124
    end_mask = col8 - (row8 + 120) <= -124
    edge_ref[72:128, :] = jnp.zeros((56, 256), F32)
    for a in range(9):
        circ = []
        for part in range(2):
            first = jnp.broadcast_to(taps_ref[part, a : a + 1, :], (128, 128))
            circ.append(pltpu.roll(first, 0, 1, stride=1, stride_axis=0))
        d_r, d_i = (jnp.where(near, m, 0.0) for m in circ)
        base = a * 256
        split_store(w_ref, pl.ds(base, 128), pl.ds(0, 128), d_r)
        split_store(w_ref, pl.ds(base, 128), pl.ds(128, 128), d_i)
        split_store(w_ref, pl.ds(base + 128, 128), pl.ds(0, 128), -d_i)
        split_store(w_ref, pl.ds(base + 128, 128), pl.ds(128, 128), d_r)
        t_r, t_i = (jnp.where(top_mask, m[0:8], 0.0) for m in circ)
        e_r, e_i = (jnp.where(end_mask, m[120:128], 0.0) for m in circ)
        rows = pl.ds(a * 8, 8)
        edge_ref[rows, 0:128] = jnp.where(
            d == 0,
            jnp.where(low, t_r, -pltpu.roll(t_i, 4, 0)),
            jnp.where(low, pltpu.roll(e_r, 4, 0), -e_i),
        )
        edge_ref[rows, 128:256] = jnp.where(
            d == 0,
            jnp.where(low, t_i, pltpu.roll(t_r, 4, 0)),
            jnp.where(low, pltpu.roll(e_i, 4, 0), e_r),
        )
    split_store(w_ref, pl.ds(2304, 128), pl.ds(0, 256), edge_ref[...])


def pack_edge(d, f_ref, out_ref):
    lane = iota((256, 128), 1)
    packed = jnp.zeros((256, 128), F32)
    for grp in range(4):
        for part in range(2):
            first = 8 * grp + 4 * part
            turned = pltpu.roll(f_ref[grp, part, 4:260, :], 4 * (1 - d) + first, 1)
            packed = jnp.where((lane >= first) & (lane < first + 4), turned, packed)
    out_ref[...] = packed.astype(BF16)


def unpack_edge(in_ref, g_ref):
    lane = iota((256, 128), 1)
    packed = in_ref[...].astype(F32)
    for grp in range(4):
        turned = pltpu.roll(packed, 128 - 8 * grp, 1) if grp else packed
        g_ref[grp, 4:260, :] = jnp.where(lane < 8, turned, 0.0)


def top_edge(d, top_ref, g_ref):
    lane = iota((256, 128), 1)
    other = pl.ds(pl.multiple_of((1 - d) * 128, 128), 128)
    for fr in range(2):
        for s in range(2):
            re = pltpu.roll(top_ref[fr, 2 * s, :, other].astype(F32), 4 * d, 1)
            im = pltpu.roll(top_ref[fr, 2 * s + 1, :, other].astype(F32), 4 + 4 * d, 1)
            g_ref[2 * fr + s, 4:260, :] = jnp.where(lane < 4, re, jnp.where(lane < 8, im, 0.0))


def edge_columns(g_ref, grp):
    edge = g_ref[grp, pl.ds(0, 256), :]
    for a in range(1, 9):
        edge = edge + pltpu.roll(g_ref[grp, pl.ds(a, 256), :], 8 * a, 1)
    return edge.astype(BF16)


def convolve(f_ref, w_ref, o_ref, fr, g_ref=None):
    fields = []
    for grp in (2 * fr, 2 * fr + 1):
        pieces = [
            f_ref[grp, part, pl.ds(a, 256), :].astype(BF16) for a in range(9) for part in range(2)
        ]
        if g_ref is not None:
            pieces.append(edge_columns(g_ref, grp))
        fields.append(jnp.concatenate(pieces, axis=1))
    left = jnp.concatenate(fields, axis=0)
    depth = slice(0, left.shape[1])
    o_ref[fr * 512 : fr * 512 + 512, :] = jnp.dot(
        left, w_ref[fr, 0, depth, :], preferred_element_type=F32
    ) + jnp.dot(left, w_ref[fr, 1, depth, :], preferred_element_type=F32)


def add_edge(g_ref, w_ref, o_ref, fr):
    left = jnp.concatenate([edge_columns(g_ref, 2 * fr), edge_columns(g_ref, 2 * fr + 1)], axis=0)
    depth = slice(2304, 2432)
    o_ref[fr * 512 : fr * 512 + 512, :] += jnp.dot(
        left, w_ref[fr, 0, depth, :], preferred_element_type=F32
    ) + jnp.dot(left, w_ref[fr, 1, depth, :], preferred_element_type=F32)


def cos_sin(angle):
    turns = jnp.round(angle * 0.6366197723675814)
    y = ((angle - turns * 1.5703125) - turns * 4.837512969970703e-4) - turns * 7.549789948768648e-8
    z = y * y
    sine = y + y * z * (-1.6666654611e-1 + z * (8.3321608736e-3 + z * -1.9515295891e-4))
    cosine = (1.0 - 0.5 * z) + z * z * (
        4.166664568298827e-2 + z * (-1.388731625493765e-3 + z * 2.443315711809948e-5)
    )
    quarter = turns.astype(jnp.int32)
    odd = (quarter & 1) == 1
    out_sine = jnp.where(odd, cosine, sine)
    out_cosine = jnp.where(odd, sine, cosine)
    return (
        jnp.where(((quarter + 1) & 2) == 2, -out_cosine, out_cosine),
        jnp.where((quarter & 2) == 2, -out_sine, out_sine),
    )


def cut_screen(slow_ref, off_x, off_y, half, wide_ref, out_ref):
    lane = iota((192, 128), 1)
    start = jnp.zeros((192, 128), jnp.int32) + (off_y + 128 * half)
    for rows in (slice(0, 192), slice(192, 384)):
        value = jnp.where(
            lane >= start,
            slow_ref[rows, 0:128],
            jnp.where(lane + 128 >= start, slow_ref[rows, 128:256], slow_ref[rows, 256:384]),
        )
        for bit in range(7):
            turned = pltpu.roll(value, 128 - (1 << bit), 1)
            value = jnp.where((start & (1 << bit)) > 0, turned, value)
        wide_ref[rows, :] = value

    @pl.loop(0, 8)
    def _(blk):
        row0 = pl.multiple_of(blk * 32, 32)
        out_ref[pl.ds(row0, 32), :] = wide_ref[pl.ds(off_x + row0, 32), :]


def apply_phase(o_ref, screen_ref, weights, f_ref):
    for fr in range(2):

        @pl.loop(0, 16)
        def _(blk):
            row0 = pl.multiple_of(blk * 16, 16)
            angle = (3.0 * weights[fr]) * screen_ref[pl.ds(row0, 16), :]
            cosine, sine = cos_sin(angle)
            for s in range(2):
                grp = fr * 2 + s
                rows = pl.ds(pl.multiple_of(grp * 256 + row0, 16), 16)
                re = o_ref[rows, 0:128]
                im = o_ref[rows, 128:256]
                f_ref[grp, 0, pl.ds(row0 + 4, 16), :] = re * cosine - im * sine
                f_ref[grp, 1, pl.ds(row0 + 4, 16), :] = re * sine + im * cosine


def flip_source(f_ref, rev_ref):
    index = 7 - iota((8, 128), 0)
    for fr in range(2):
        for part in range(2):
            for t in range(33):
                rev_ref[fr, part, 8 * (32 - t) : 8 * (32 - t) + 8, :] = jnp.take_along_axis(
                    f_ref[fr * 2, part, 8 * t : 8 * t + 8, :], index, axis=0
                )


def image_piece(f_ref, rev_ref, img_ref, xx):
    @pl.loop(0, NZ)
    def _(z):
        blk = z * NXX + xx
        row0 = pl.multiple_of(blk * 8, 8)
        rev0 = pl.multiple_of(248 - blk * 8, 8)
        for j in range(8):
            s_rows = pl.ds(rev0 + (7 - j), 8)
            r_rows = pl.ds(row0 + j, 8)
            value = jnp.zeros((8, 128), F32)
            for fr in range(2):
                for part in range(2):
                    value = value + rev_ref[fr, part, s_rows, :] * f_ref[fr * 2 + 1, part, r_rows, :]
            to = pl.multiple_of((j // 4) * 128 + z * 16 + (j % 2) * 8, 8)
            img_ref[(j // 2) % 2, xx, pl.ds(to, 8), :] = value


def kernel(
    total,
    offsets_ref, taps_ref, slow_hbm, top_hbm, out_ref,
    slow_ref, top_ref, f_ref, g_ref, w_ref, edge_ref, o_ref, rev_ref, pad_ref, wide_ref,
    taps_all, screens, screen_tx, edge_tx, edge_rx, img, rx1, tx2, rx2, acc, tx3, rx3,
    local_sem, s0_send, s0_recv, s1_send, s1_recv, s2_send, s2_recv, s3_send, s3_recv,
):
    d = lax.axis_index("depth")
    f = lax.axis_index("freq")
    core, yhi, xx, z = f % 2, (f // 2) % 2, (f // 4) % NXX, f // 16

    load_top = pltpu.make_async_copy(top_hbm, top_ref, local_sem.at[0])
    load_slow = pltpu.make_async_copy(slow_hbm, slow_ref, local_sem.at[1])

    def device(depth=d, zc=z, xc=xx, yc=yhi, cc=core):
        return (depth, ((zc * NXX + xc) * 2 + yc) * 2 + cc)

    xs, ys = [(xx + off) % NXX for off in range(NXX)], [yhi, 1 - yhi]
    z_peers = [device(zc=(z + off) % NZ) for off in range(1, NZ)]
    core_peer = device(cc=1 - core)
    depth_peer = device(depth=1 - d)
    plane = [
        device(depth=(d + rel) % 2, xc=xs[xo], yc=ys[yo])
        for rel in range(2) for xo in range(NXX) for yo in range(2)
    ][1:]
    everyone = [core_peer] + plane + z_peers
    barrier = pltpu.get_barrier_semaphore()
    for peer in everyone:
        pl.semaphore_signal(barrier, inc=1, device_id=peer, device_id_type=MESH)
    load_slow.start()
    load_top.start()

    def remote(src, dst, send, recv, peer):
        return pltpu.make_async_remote_copy(
            src_ref=src, dst_ref=dst, send_sem=send, recv_sem=recv,
            device_id=peer, device_id_type=MESH,
        )

    swap_taps = remote(taps_all.at[d], taps_all.at[d], s0_send.at[0], s0_recv.at[0], depth_peer)
    swap_screen = remote(screen_tx, screens.at[d], s0_send.at[1], s0_recv.at[1], depth_peer)
    swap_edge = remote(edge_tx, edge_rx, s0_send.at[2], s0_recv.at[2], depth_peer)
    weights = [(2 * f + fr + 1).astype(F32) / total for fr in range(2)]

    def stage1_copy(k, off):
        return remote(
            img.at[k, 1 - core, xs[off]], rx1.at[k, off],
            s1_send.at[k, off], s1_recv.at[k, off], core_peer,
        )

    def stage2_copy(k, xo, yo):
        at = ((d + k) % 2) * 8 + xo * 2 + yo
        return remote(
            tx2.at[k, xo * 2 + yo], rx2.at[k, at], s2_send.at[k, xo * 2 + yo], s2_recv.at[k, at],
            device(depth=k, xc=xs[xo], yc=ys[yo]),
        )

    def stage2_get(k, at):
        return remote(rx2.at[k, at], rx2.at[k, at], s2_send.at[k, 0], s2_recv.at[k, at], depth_peer)

    def stage3_copy(k, off):
        return remote(
            tx3.at[k, off - 1], rx3.at[k, off - 1],
            s3_send.at[k, off - 1], s3_recv.at[k, off - 1], z_peers[off - 1],
        )

    def make_image(k):
        flip_source(f_ref, rev_ref)
        for off in X_ORDER:
            image_piece(f_ref, rev_ref, img.at[k], xs[off])
            stage1_copy(k, off).start()

    def after_core(k):
        for off in X_ORDER:
            stage1_copy(k, off).wait_recv()
            for yo in (1, 0):
                rows = pl.ds(pl.multiple_of(ys[yo] * 128, 128), 128)
                value = img[k, core, xs[off], rows, :] + rx1[k, off, rows, :]
                if off == 0 and yo == 0:
                    acc[k] = value
                tx2[k, off * 2 + yo] = value.astype(BF16)
                if off == 0 and yo == 0:

                    @pl.when(d != k)
                    def _():
                        stage2_copy(k, 0, 0).start()
                else:
                    stage2_copy(k, off, yo).start()

    def after_plane(k):
        @pl.when(d == k)
        def _():
            for at in range(1, 16):
                stage2_get(k, at).wait_recv()

            def total_of(part):
                rows = pl.ds(pl.multiple_of(part * 16, 16), 16)
                near = acc[k, rows, :]
                for at in range(1, 8):
                    near = near + rx2[k, at, rows, :].astype(F32)
                far = rx2[k, 8, rows, :].astype(F32)
                for at in range(9, 16):
                    far = far + rx2[k, at, rows, :].astype(F32)
                return jnp.concatenate([near, far], axis=0)

            for off in (4, 3, 5, 2, 6, 1, 7):
                tx3[k, off - 1] = total_of((z + off) % NZ).astype(BF16)
                stage3_copy(k, off).start()
            acc[k, 0:32, :] = total_of(z)

    def after_z(k):
        @pl.when(d == k)
        def _():
            for off in range(1, NZ):
                stage3_copy(k, off).wait_recv()
            value = acc[k, 0:32, :]
            for off in range(1, NZ):
                value = value + rx3[k, off - 1].astype(F32)
            for half in range(2):
                lanes = k * 128 if half == 0 else (1 - k) * 128
                for low in range(2):
                    rows = slice(half * 16 + low * 8, half * 16 + low * 8 + 8)
                    out_ref[:, pl.ds(low * 256 + lanes, 128)] = value[rows]

    arrange_taps(taps_ref, pad_ref, taps_all.at[d])
    pl.semaphore_wait(barrier, len(everyone))
    swap_taps.start()
    f_ref[:, :, 0:8, :] = jnp.zeros((4, 2, 8, 128), F32)
    f_ref[:, :, 256:264, :] = jnp.zeros((4, 2, 8, 128), F32)
    g_ref[:, 0:8, :] = jnp.zeros((4, 8, 128), F32)
    g_ref[:, 256:264, :] = jnp.zeros((4, 8, 128), F32)
    off_x, off_y = offsets_ref[0, 0], offsets_ref[0, 1]
    load_slow.wait()
    cut_screen(slow_ref, off_x, off_y, 1 - d, wide_ref, screen_tx)
    swap_screen.start()
    load_top.wait()
    mine = pl.ds(pl.multiple_of(d * 128, 128), 128)
    for fr in range(2):
        for s in range(2):
            for part in range(2):
                f_ref[fr * 2 + s, part, 4:260, :] = top_ref[fr, 2 * s + part, :, mine].astype(F32)
    top_edge(d, top_ref, g_ref)
    cut_screen(slow_ref, off_x, off_y, d, wide_ref, screens.at[d])

    swap_taps.wait_recv()
    for fr in range(2):
        build_weights(d, taps_all.at[0, fr], w_ref.at[0, fr], edge_ref.at[0])
    for fr in range(2):
        convolve(f_ref, w_ref.at[0], o_ref, fr, g_ref)
        build_weights(d, taps_all.at[1, fr], w_ref.at[1, fr], edge_ref.at[1])
    swap_screen.wait_recv()
    apply_phase(o_ref, screens.at[0], weights, f_ref)
    pack_edge(d, f_ref, edge_tx)
    swap_edge.start()
    make_image(0)
    for fr in range(2):
        convolve(f_ref, w_ref.at[1], o_ref, fr)
    after_core(0)
    swap_edge.wait_recv()
    unpack_edge(edge_rx, g_ref)
    for fr in range(2):
        add_edge(g_ref, w_ref.at[1], o_ref, fr)
    apply_phase(o_ref, screens.at[1], weights, f_ref)
    make_image(1)
    after_core(1)
    after_plane(0)
    after_z(0)
    after_plane(1)
    after_z(1)

    swap_taps.wait_send()
    swap_screen.wait_send()
    swap_edge.wait_send()
    for k in range(2):
        for off in range(NXX):
            stage1_copy(k, off).wait_send()
            for yo in range(2):
                if off or yo:
                    stage2_copy(k, off, yo).wait_send()

        @pl.when(d != k)
        def _():
            stage2_copy(k, 0, 0).wait_send()

        @pl.when(d == k)
        def _():
            for off in range(1, NZ):
                stage3_copy(k, off).wait_send()


def migrate(total, offsets, taps, slowness, top):
    dma = pltpu.SemaphoreType.DMA
    vmem = pl.BlockSpec(memory_space=pltpu.VMEM)
    hbm = pl.BlockSpec(memory_space=pl.ANY)
    return pl.pallas_call(
        functools.partial(kernel, total),
        out_shape=jax.ShapeDtypeStruct((8, 512), F32),
        in_specs=[pl.BlockSpec(memory_space=pltpu.SMEM), vmem, hbm, hbm],
        out_specs=vmem,
        scratch_shapes=[
            pltpu.VMEM((384, 384), F32),
            pltpu.VMEM((2, 4, 256, 256), BF16),
            pltpu.VMEM((4, 2, 264, 128), F32),
            pltpu.VMEM((4, 264, 128), F32),
            pltpu.VMEM((2, 2, 2, 2432, 256), BF16),
            pltpu.VMEM((2, 128, 256), F32),
            pltpu.VMEM((1024, 256), F32),
            pltpu.VMEM((2, 2, 264, 128), F32),
            pltpu.VMEM((8, 128), F32),
            pltpu.VMEM((384, 128), F32),
            pltpu.VMEM((2, 2, 2, 16, 128), F32),
            pltpu.VMEM((2, 256, 128), F32),
            pltpu.VMEM((256, 128), F32),
            pltpu.VMEM((256, 128), BF16),
            pltpu.VMEM((256, 128), BF16),
            pltpu.VMEM((2, 2, NXX, 256, 128), F32),
            pltpu.VMEM((2, NXX, 256, 128), F32),
            pltpu.VMEM((2, 8, 128, 128), BF16),
            pltpu.VMEM((2, 16, 128, 128), BF16),
            pltpu.VMEM((2, 128, 128), F32),
            pltpu.VMEM((2, 7, 32, 128), BF16),
            pltpu.VMEM((2, 7, 32, 128), BF16),
            dma((2,)), dma((3,)), dma((3,)), dma((2, 4)), dma((2, 4)), dma((2, 8)), dma((2, 16)),
            dma((2, 7)), dma((2, 7)),
        ],
        compiler_params=pltpu.CompilerParams(
            collective_id=0, has_side_effects=True, vmem_limit_bytes=56 * 2**20
        ),
    )(offsets, taps, slowness, top)


def local(total, top_fields, slowness, kernels, offsets):
    out = migrate(float(total), offsets, kernels[0], slowness[0], top_fields[0])
    return out[None, None] * float(total) ** -0.5


def solution(mesh):
    return jax.shard_map(
        functools.partial(local, 256),
        mesh=mesh,
        in_specs=(
            P(None, "freq", None, None, None),
            P("depth", None, None),
            P("depth", "freq", None, None),
            P(),
        ),
        out_specs=P("depth", None, None, "freq"),
        check_vma=False,
    )
```

```python
import functools

import jax
import jax.numpy as jnp
from jax import lax
from jax.experimental import pallas as pl
from jax.experimental.pallas import tpu as pltpu
from jax.sharding import PartitionSpec as P

F32, BF16 = jnp.float32, jnp.bfloat16
MESH = pl.DeviceIdType.MESH

NZ, NXX = 8, 4
X_ORDER = (2, 1, 3, 0)


def iota(shape, dim):
    return lax.broadcasted_iota(jnp.int32, shape, dim)


def split_store(w_ref, rows, cols, value):
    high = value.astype(BF16)
    w_ref[0, rows, cols] = high
    w_ref[1, rows, cols] = (value - high.astype(F32)).astype(BF16)


def arrange_taps(taps_ref, pad_ref, out_ref):
    lane, row = iota((8, 128), 1), iota((8, 128), 0)
    used = (lane < 5) | (lane >= 124)
    place = jnp.where(lane < 5, 4 - lane, 132 - lane)
    pad_ref[...] = jnp.zeros_like(pad_ref)
    for fr in range(2):
        for part in range(2):
            pad_ref[2 * fr + part : 2 * fr + part + 1, 0:81] = taps_ref[fr, part : part + 1, :]
    for fr in range(2):
        for part in range(2):
            line = jnp.broadcast_to(pad_ref[2 * fr + part : 2 * fr + part + 1, :], (8, 128))
            for half in range(2):
                index = jnp.where(used, jnp.minimum(9 * (row + 8 * half), 72) + place, 127)
                out_ref[fr, part, 8 * half : 8 * half + 8, :] = jnp.take_along_axis(line, index, axis=1)


def build_weights(d, taps_ref, w_ref, edge_ref):
    row, col = iota((128, 128), 0), iota((128, 128), 1)
    near = jnp.abs(col - row) <= 4
    row8, col8 = iota((8, 128), 0), iota((8, 128), 1)
    low = row8 < 4
    top_mask = col8 - row8 >= 124
    end_mask = col8 - (row8 + 120) <= -124
    edge_ref[72:128, :] = jnp.zeros((56, 256), F32)
    for a in range(9):
        circ = []
        for part in range(2):
            first = jnp.broadcast_to(taps_ref[part, a : a + 1, :], (128, 128))
            circ.append(pltpu.roll(first, 0, 1, stride=1, stride_axis=0))
        d_r, d_i = (jnp.where(near, m, 0.0) for m in circ)
        base = a * 256
        split_store(w_ref, pl.ds(base, 128), pl.ds(0, 128), d_r)
        split_store(w_ref, pl.ds(base, 128), pl.ds(128, 128), d_i)
        split_store(w_ref, pl.ds(base + 128, 128), pl.ds(0, 128), -d_i)
        split_store(w_ref, pl.ds(base + 128, 128), pl.ds(128, 128), d_r)
        t_r, t_i = (jnp.where(top_mask, m[0:8], 0.0) for m in circ)
        e_r, e_i = (jnp.where(end_mask, m[120:128], 0.0) for m in circ)
        rows = pl.ds(a * 8, 8)
        edge_ref[rows, 0:128] = jnp.where(
            d == 0,
            jnp.where(low, t_r, -pltpu.roll(t_i, 4, 0)),
            jnp.where(low, pltpu.roll(e_r, 4, 0), -e_i),
        )
        edge_ref[rows, 128:256] = jnp.where(
            d == 0,
            jnp.where(low, t_i, pltpu.roll(t_r, 4, 0)),
            jnp.where(low, pltpu.roll(e_i, 4, 0), e_r),
        )
    split_store(w_ref, pl.ds(2304, 128), pl.ds(0, 256), edge_ref[...])


def pack_edge(d, f_ref, out_ref):
    lane = iota((64, 128), 1)
    packed = jnp.zeros((64, 128), F32)
    for quarter in range(4):
        rows = slice(4 + 64 * quarter, 68 + 64 * quarter)
        for grp in range(4):
            for part in range(2):
                first = 32 * quarter + 8 * grp + 4 * part
                turned = pltpu.roll(f_ref[grp, part, rows, :], 4 * (1 - d) + first, 1)
                packed = jnp.where((lane >= first) & (lane < first + 4), turned, packed)
    out_ref[...] = packed.astype(BF16)


def unpack_edge(in_ref, wide_ref, turned_ref):
    lane = iota((64, 128), 1)
    packed = in_ref[...].astype(F32)
    wide_ref[0:8, :] = jnp.zeros((8, 128), F32)
    wide_ref[256:264, :] = jnp.zeros((8, 128), F32)
    for quarter in range(4):
        turned = pltpu.roll(packed, 128 - 32 * quarter, 1) if quarter else packed
        wide_ref[4 + 64 * quarter : 68 + 64 * quarter, :] = jnp.where(lane < 32, turned, 0.0)
    wide = wide_ref[0:264, :]
    for n in range(12):
        turned_ref[n] = pltpu.roll(wide, (8 * (n - 3)) % 128, 1) if n != 3 else wide


def top_edge(d, top_ref, g_ref):
    lane = iota((256, 128), 1)
    other = pl.ds(pl.multiple_of((1 - d) * 128, 128), 128)
    for fr in range(2):
        for s in range(2):
            re = pltpu.roll(top_ref[fr, 2 * s, :, other].astype(F32), 4 * d, 1)
            im = pltpu.roll(top_ref[fr, 2 * s + 1, :, other].astype(F32), 4 + 4 * d, 1)
            g_ref[2 * fr + s, 4:260, :] = jnp.where(lane < 4, re, jnp.where(lane < 8, im, 0.0))


def edge_columns(g_ref, grp):
    edge = g_ref[grp, pl.ds(0, 256), :]
    for a in range(1, 9):
        edge = edge + pltpu.roll(g_ref[grp, pl.ds(a, 256), :], 8 * a, 1)
    return edge.astype(BF16)


def convolve(f_ref, w_ref, o_ref, fr, g_ref=None):
    fields = []
    for grp in (2 * fr, 2 * fr + 1):
        pieces = [
            f_ref[grp, part, pl.ds(a, 256), :].astype(BF16) for a in range(9) for part in range(2)
        ]
        if g_ref is not None:
            pieces.append(edge_columns(g_ref, grp))
        fields.append(jnp.concatenate(pieces, axis=1))
    left = jnp.concatenate(fields, axis=0)
    depth = slice(0, left.shape[1])
    o_ref[fr * 512 : fr * 512 + 512, :] = jnp.dot(
        left, w_ref[fr, 0, depth, :], preferred_element_type=F32
    ) + jnp.dot(left, w_ref[fr, 1, depth, :], preferred_element_type=F32)


def add_edge(turned_ref, w_ref, o_ref):
    lane = iota((256, 128), 1)
    for fr in range(2):
        fields = []
        for grp in (2 * fr, 2 * fr + 1):
            edge = jnp.zeros((256, 128), F32)
            for a in range(9):
                here = (lane >= 8 * a) & (lane < 8 * a + 8)
                edge = jnp.where(here, turned_ref[a - grp + 3, pl.ds(a, 256), :], edge)
            fields.append(edge.astype(BF16))
        left = jnp.concatenate(fields, axis=0)
        depth = slice(2304, 2432)
        o_ref[fr * 512 : fr * 512 + 512, :] += jnp.dot(
            left, w_ref[fr, 0, depth, :], preferred_element_type=F32
        ) + jnp.dot(left, w_ref[fr, 1, depth, :], preferred_element_type=F32)


def cos_sin(angle):
    turns = jnp.round(angle * 0.6366197723675814)
    y = ((angle - turns * 1.5703125) - turns * 4.837512969970703e-4) - turns * 7.549789948768648e-8
    z = y * y
    sine = y + y * z * (-1.6666654611e-1 + z * (8.3321608736e-3 + z * -1.9515295891e-4))
    cosine = (1.0 - 0.5 * z) + z * z * (
        4.166664568298827e-2 + z * (-1.388731625493765e-3 + z * 2.443315711809948e-5)
    )
    quarter = turns.astype(jnp.int32)
    odd = (quarter & 1) == 1
    out_sine = jnp.where(odd, cosine, sine)
    out_cosine = jnp.where(odd, sine, cosine)
    return (
        jnp.where(((quarter + 1) & 2) == 2, -out_cosine, out_cosine),
        jnp.where((quarter & 2) == 2, -out_sine, out_sine),
    )


def cut_screen(slow_ref, off_x, off_y, sides, wide_ref, outs):
    value = slow_ref[...]
    high = value.astype(BF16)
    rest = value - high.astype(F32)
    middle = rest.astype(BF16)
    low = (rest - middle.astype(F32)).astype(BF16)
    lane = iota((384, 256), 1)
    column = jnp.where(lane < 128, lane + 128 * sides[0], lane - 128 + 128 * sides[1]) + off_y
    pick = jnp.where(iota((384, 256), 0) == column, 1.0, 0.0).astype(BF16)
    high, middle, low = (
        jnp.dot(part, pick, preferred_element_type=F32) for part in (high, middle, low)
    )
    moved = high + (middle + low)
    wide_ref[0] = moved[:, 0:128]
    wide_ref[1] = moved[:, 128:256]
    for side in range(2):
        outs[side][...] = wide_ref[side, pl.ds(off_x, 256), :]


def apply_phase(o_ref, screen_ref, weights, f_ref):
    for fr in range(2):

        @pl.loop(0, 4)
        def _(blk):
            row0 = pl.multiple_of(blk * 64, 64)
            angle = (3.0 * weights[fr]) * screen_ref[pl.ds(row0, 64), :]
            cosine, sine = cos_sin(angle)
            for s in range(2):
                grp = fr * 2 + s
                rows = pl.ds(pl.multiple_of(grp * 256 + row0, 64), 64)
                re = o_ref[rows, 0:128]
                im = o_ref[rows, 128:256]
                f_ref[grp, 0, pl.ds(row0 + 4, 64), :] = re * cosine - im * sine
                f_ref[grp, 1, pl.ds(row0 + 4, 64), :] = re * sine + im * cosine


def flip_source(f_ref, rev_ref):
    index = 7 - iota((8, 128), 0)
    for fr in range(2):
        for part in range(2):
            for t in range(33):
                rev_ref[fr, part, 8 * (32 - t) : 8 * (32 - t) + 8, :] = jnp.take_along_axis(
                    f_ref[fr * 2, part, 8 * t : 8 * t + 8, :], index, axis=0
                )


def image_piece(f_ref, rev_ref, img_ref, xx):
    @pl.loop(0, NZ)
    def _(z):
        blk = z * NXX + xx
        row0 = pl.multiple_of(blk * 8, 8)
        rev0 = pl.multiple_of(248 - blk * 8, 8)
        for j in range(8):
            s_rows = pl.ds(rev0 + (7 - j), 8)
            r_rows = pl.ds(row0 + j, 8)
            value = jnp.zeros((8, 128), F32)
            for fr in range(2):
                for part in range(2):
                    value = value + rev_ref[fr, part, s_rows, :] * f_ref[fr * 2 + 1, part, r_rows, :]
            to = pl.multiple_of((j // 4) * 128 + z * 16 + (j % 2) * 8, 8)
            img_ref[(j // 2) % 2, xx, pl.ds(to, 8), :] = value


def kernel(
    total,
    offsets_ref, taps_ref, slow_hbm, top_hbm, out_ref,
    slow_ref, top_ref, f_ref, g_ref, w_ref, edge_ref, o_ref, rev_ref, pad_ref, wide_ref, cut_ref,
    taps_all, screens, screen_tx, turned_ref, edge_tx, edge_rx, img, rx1, tx2, rx2, acc, tx3, rx3, own_part,
    local_sem, s0_send, s0_recv, s1_send, s1_recv, s2_send, s2_recv, s3_send, s3_recv,
):
    d = lax.axis_index("depth")
    f = lax.axis_index("freq")
    core, yhi, xx, z = f % 2, (f // 2) % 2, (f // 4) % NXX, f // 16

    load_top = pltpu.make_async_copy(top_hbm, top_ref, local_sem.at[0])
    load_slow = pltpu.make_async_copy(slow_hbm, slow_ref, local_sem.at[1])

    def device(depth=d, zc=z, xc=xx, yc=yhi, cc=core):
        return (depth, ((zc * NXX + xc) * 2 + yc) * 2 + cc)

    xs, ys = [(xx + off) % NXX for off in range(NXX)], [yhi, 1 - yhi]
    z_peers = [device(zc=(z + off) % NZ) for off in range(1, NZ)]
    core_peer = device(cc=1 - core)
    depth_peer = device(depth=1 - d)
    plane = [
        device(depth=(d + rel) % 2, xc=xs[xo], yc=ys[yo])
        for rel in range(2) for xo in range(NXX) for yo in range(2)
    ][1:]
    everyone = [core_peer] + plane + z_peers
    barrier = pltpu.get_barrier_semaphore()
    for peer in everyone:
        pl.semaphore_signal(barrier, inc=1, device_id=peer, device_id_type=MESH)
    load_slow.start()
    load_top.start()

    def remote(src, dst, send, recv, peer):
        return pltpu.make_async_remote_copy(
            src_ref=src, dst_ref=dst, send_sem=send, recv_sem=recv,
            device_id=peer, device_id_type=MESH,
        )

    swap_taps = remote(taps_all.at[d], taps_all.at[d], s0_send.at[0], s0_recv.at[0], depth_peer)
    swap_screen = remote(screen_tx, screens.at[d], s0_send.at[1], s0_recv.at[1], depth_peer)
    swap_edge = remote(edge_tx, edge_rx, s0_send.at[2], s0_recv.at[2], depth_peer)
    weights = [(2 * f + fr + 1).astype(F32) / total for fr in range(2)]

    def stage1_copy(k, off):
        return remote(
            img.at[k, 1 - core, xs[off]], rx1.at[k, off],
            s1_send.at[k, off], s1_recv.at[k, off], core_peer,
        )

    def stage2_copy(k, xo, yo, part):
        at = ((d + k) % 2) * 8 + xo * 2 + yo
        rows = pl.ds(part * 64, 64)
        return remote(
            tx2.at[k, xo * 2 + yo, rows], rx2.at[k, at, rows],
            s2_send.at[k, part, xo * 2 + yo], s2_recv.at[k, part, at],
            device(depth=k, xc=xs[xo], yc=ys[yo]),
        )

    def stage2_get(k, at, part):
        here = rx2.at[k, at, pl.ds(part * 64, 64)]
        return remote(here, here, s2_send.at[k, part, 0], s2_recv.at[k, part, at], depth_peer)

    def stage3_copy(k, to):
        off = (to - z + NZ) % NZ
        return remote(
            tx3.at[k, to], rx3.at[k, off], s3_send.at[k, to], s3_recv.at[k, off], device(zc=to)
        )

    def stage3_get(k, off):
        return remote(
            rx3.at[k, off], rx3.at[k, off], s3_send.at[k, 0], s3_recv.at[k, off], depth_peer
        )

    def make_image(k):
        flip_source(f_ref, rev_ref)
        for off in X_ORDER:
            image_piece(f_ref, rev_ref, img.at[k], xs[off])
            stage1_copy(k, off).start()

    def after_core(k):
        for off in X_ORDER:
            stage1_copy(k, off).wait_recv()
            for yo in (1, 0):
                rows = pl.ds(pl.multiple_of(ys[yo] * 128, 128), 128)
                value = img[k, core, xs[off], rows, :] + rx1[k, off, rows, :]
                if off == 0 and yo == 0:
                    acc[k] = value
                tx2[k, off * 2 + yo] = value.astype(BF16)
                if off or yo:
                    stage2_copy(k, off, yo, 0).start()
        for off in X_ORDER:
            for yo in (1, 0):
                if off or yo:
                    stage2_copy(k, off, yo, 1).start()

        @pl.when(d != k)
        def _():
            for part in range(2):
                stage2_copy(k, 0, 0, part).start()

    def after_plane(k):
        @pl.when(d == k)
        def _():
            for part in range(2):
                for at in range(1, 16):
                    stage2_get(k, at, part).wait_recv()
                for to in range(4 * part, 4 * part + 4):
                    rows = pl.ds(to * 16, 16)
                    near = acc[k, rows, :]
                    for at in range(1, 8):
                        near = near + rx2[k, at, rows, :].astype(F32)
                    far = rx2[k, 8, rows, :].astype(F32)
                    for at in range(9, 16):
                        far = far + rx2[k, at, rows, :].astype(F32)
                    value = jnp.concatenate([near, far], axis=0)
                    tx3[k, to] = value.astype(BF16)

                    @pl.when(z != to)
                    def _():
                        stage3_copy(k, to).start()

                    @pl.when(z == to)
                    def _():
                        own_part[k] = value

    def after_z(k):
        @pl.when(d == k)
        def _():
            for off in range(1, NZ):
                stage3_get(k, off).wait_recv()
            value = own_part[k]
            for off in range(1, NZ):
                value = value + rx3[k, off].astype(F32)
            for half in range(2):
                lanes = k * 128 if half == 0 else (1 - k) * 128
                for low in range(2):
                    rows = slice(half * 16 + low * 8, half * 16 + low * 8 + 8)
                    out_ref[:, pl.ds(low * 256 + lanes, 128)] = value[rows]

    arrange_taps(taps_ref, pad_ref, taps_all.at[d])
    pl.semaphore_wait(barrier, len(everyone))
    swap_taps.start()
    f_ref[:, :, 0:8, :] = jnp.zeros((4, 2, 8, 128), F32)
    f_ref[:, :, 256:264, :] = jnp.zeros((4, 2, 8, 128), F32)
    g_ref[:, 0:8, :] = jnp.zeros((4, 8, 128), F32)
    g_ref[:, 256:264, :] = jnp.zeros((4, 8, 128), F32)
    off_x, off_y = offsets_ref[0, 0], offsets_ref[0, 1]
    load_slow.wait()
    cut_screen(slow_ref, off_x, off_y, (1 - d, d), cut_ref, (screen_tx, screens.at[d]))
    swap_screen.start()
    load_top.wait()
    mine = pl.ds(pl.multiple_of(d * 128, 128), 128)
    for fr in range(2):
        for s in range(2):
            for part in range(2):
                f_ref[fr * 2 + s, part, 4:260, :] = top_ref[fr, 2 * s + part, :, mine].astype(F32)
    top_edge(d, top_ref, g_ref)

    swap_taps.wait_recv()
    for fr in range(2):
        build_weights(d, taps_all.at[0, fr], w_ref.at[0, fr], edge_ref.at[0])
    for fr in range(2):
        convolve(f_ref, w_ref.at[0], o_ref, fr, g_ref)
        build_weights(d, taps_all.at[1, fr], w_ref.at[1, fr], edge_ref.at[1])
    swap_screen.wait_recv()
    apply_phase(o_ref, screens.at[0], weights, f_ref)
    pack_edge(d, f_ref, edge_tx)
    swap_edge.start()
    make_image(0)
    for fr in range(2):
        convolve(f_ref, w_ref.at[1], o_ref, fr)
    after_core(0)
    swap_edge.wait_recv()
    unpack_edge(edge_rx, wide_ref, turned_ref)
    add_edge(turned_ref, w_ref.at[1], o_ref)
    apply_phase(o_ref, screens.at[1], weights, f_ref)
    make_image(1)
    after_core(1)
    after_plane(0)
    after_z(0)
    after_plane(1)
    after_z(1)

    swap_taps.wait_send()
    swap_screen.wait_send()
    swap_edge.wait_send()
    for k in range(2):
        for off in range(NXX):
            stage1_copy(k, off).wait_send()
            for yo in range(2):
                if off or yo:
                    for part in range(2):
                        stage2_copy(k, off, yo, part).wait_send()

        @pl.when(d != k)
        def _():
            for part in range(2):
                stage2_copy(k, 0, 0, part).wait_send()

        @pl.when(d == k)
        def _():
            for to in range(NZ):

                @pl.when(z != to)
                def _():
                    stage3_copy(k, to).wait_send()


def migrate(total, offsets, taps, slowness, top):
    dma = pltpu.SemaphoreType.DMA
    vmem = pl.BlockSpec(memory_space=pltpu.VMEM)
    hbm = pl.BlockSpec(memory_space=pl.ANY)
    return pl.pallas_call(
        functools.partial(kernel, total),
        out_shape=pltpu.VMEM((8, 512), F32),
        in_specs=[pl.BlockSpec(memory_space=pltpu.SMEM), vmem, hbm, hbm],
        out_specs=vmem,
        scratch_shapes=[
            pltpu.VMEM((384, 384), F32),
            pltpu.VMEM((2, 4, 256, 256), BF16),
            pltpu.VMEM((4, 2, 264, 128), F32),
            pltpu.VMEM((4, 264, 128), F32),
            pltpu.VMEM((2, 2, 2, 2432, 256), BF16),
            pltpu.VMEM((2, 128, 256), F32),
            pltpu.VMEM((1024, 256), F32),
            pltpu.VMEM((2, 2, 264, 128), F32),
            pltpu.VMEM((8, 128), F32),
            pltpu.VMEM((384, 128), F32),
            pltpu.VMEM((2, 384, 128), F32),
            pltpu.VMEM((2, 2, 2, 16, 128), F32),
            pltpu.VMEM((2, 256, 128), F32),
            pltpu.VMEM((256, 128), F32),
            pltpu.VMEM((12, 264, 128), F32),
            pltpu.VMEM((64, 128), BF16),
            pltpu.VMEM((64, 128), BF16),
            pltpu.VMEM((2, 2, NXX, 256, 128), F32),
            pltpu.VMEM((2, NXX, 256, 128), F32),
            pltpu.VMEM((2, 8, 128, 128), BF16),
            pltpu.VMEM((2, 16, 128, 128), BF16),
            pltpu.VMEM((2, 128, 128), F32),
            pltpu.VMEM((2, 8, 32, 128), BF16),
            pltpu.VMEM((2, 8, 32, 128), BF16),
            pltpu.VMEM((2, 32, 128), F32),
            dma((2,)), dma((3,)), dma((3,)), dma((2, 4)), dma((2, 4)), dma((2, 2, 8)), dma((2, 2, 16)),
            dma((2, 8)), dma((2, 8)),
        ],
        compiler_params=pltpu.CompilerParams(
            collective_id=0, has_side_effects=True, vmem_limit_bytes=56 * 2**20
        ),
    )(offsets, taps, slowness, top)


def local(total, top_fields, slowness, kernels, offsets):
    out = migrate(float(total), offsets, kernels[0], slowness[0], top_fields[0])
    return out[None, None] * float(total) ** -0.5


def solution(mesh):
    return jax.shard_map(
        functools.partial(local, 256),
        mesh=mesh,
        in_specs=(
            P(None, "freq", None, None, None),
            P("depth", None, None),
            P("depth", "freq", None, None),
            P(),
        ),
        out_specs=P("depth", None, None, "freq"),
        check_vma=False,
    )
```

```python
import functools

import jax
import jax.numpy as jnp
from jax import lax
from jax.experimental import pallas as pl
from jax.experimental.pallas import tpu as pltpu
from jax.sharding import PartitionSpec as P

F32, BF16 = jnp.float32, jnp.bfloat16
MESH = pl.DeviceIdType.MESH

NZ, NXX = 8, 4
X_ORDER = (2, 1, 3, 0)
ALL, UPPER, LOWER = (0, 256), (0, 144), (144, 112)
PARTS = (((0, 2),), ((0, 1), (1, 1)))


def iota(shape, dim):
    return lax.broadcasted_iota(jnp.int32, shape, dim)


def split_store(w_ref, rows, cols, value):
    high = value.astype(BF16)
    w_ref[0, rows, cols] = high
    w_ref[1, rows, cols] = (value - high.astype(F32)).astype(BF16)


def arrange_taps(taps_ref, pad_ref, out_ref):
    lane, row = iota((8, 128), 1), iota((8, 128), 0)
    used = (lane < 5) | (lane >= 124)
    place = jnp.where(lane < 5, 4 - lane, 132 - lane)
    pad_ref[...] = jnp.zeros_like(pad_ref)
    for fr in range(2):
        for part in range(2):
            pad_ref[2 * fr + part : 2 * fr + part + 1, 0:81] = taps_ref[fr, part : part + 1, :]
    for fr in range(2):
        for part in range(2):
            line = jnp.broadcast_to(pad_ref[2 * fr + part : 2 * fr + part + 1, :], (8, 128))
            for half in range(2):
                index = jnp.where(used, jnp.minimum(9 * (row + 8 * half), 72) + place, 127)
                out_ref[fr, part, 8 * half : 8 * half + 8, :] = jnp.take_along_axis(line, index, axis=1)


def build_weights(d, taps_ref, w_ref, edge_ref):
    row, col = iota((128, 128), 0), iota((128, 128), 1)
    near = jnp.abs(col - row) <= 4
    row8, col8 = iota((8, 128), 0), iota((8, 128), 1)
    low = row8 < 4
    top_mask = col8 - row8 >= 124
    end_mask = col8 - (row8 + 120) <= -124
    edge_ref[72:128, :] = jnp.zeros((56, 256), F32)
    for a in range(9):
        circ = []
        for part in range(2):
            first = jnp.broadcast_to(taps_ref[part, a : a + 1, :], (128, 128))
            circ.append(pltpu.roll(first, 0, 1, stride=1, stride_axis=0))
        d_r, d_i = (jnp.where(near, m, 0.0) for m in circ)
        base = a * 256
        split_store(w_ref, pl.ds(base, 128), pl.ds(0, 128), d_r)
        split_store(w_ref, pl.ds(base, 128), pl.ds(128, 128), d_i)
        split_store(w_ref, pl.ds(base + 128, 128), pl.ds(0, 128), -d_i)
        split_store(w_ref, pl.ds(base + 128, 128), pl.ds(128, 128), d_r)
        t_r, t_i = (jnp.where(top_mask, m[0:8], 0.0) for m in circ)
        e_r, e_i = (jnp.where(end_mask, m[120:128], 0.0) for m in circ)
        rows = pl.ds(a * 8, 8)
        edge_ref[rows, 0:128] = jnp.where(
            d == 0,
            jnp.where(low, t_r, -pltpu.roll(t_i, 4, 0)),
            jnp.where(low, pltpu.roll(e_r, 4, 0), -e_i),
        )
        edge_ref[rows, 128:256] = jnp.where(
            d == 0,
            jnp.where(low, t_i, pltpu.roll(t_r, 4, 0)),
            jnp.where(low, pltpu.roll(e_i, 4, 0), e_r),
        )
    split_store(w_ref, pl.ds(2304, 128), pl.ds(0, 256), edge_ref[...])


def pack_edge(d, f_ref, out_ref):
    lane = iota((64, 128), 1)
    packed = jnp.zeros((64, 128), F32)
    for quarter in range(4):
        rows = slice(4 + 64 * quarter, 68 + 64 * quarter)
        for grp in range(4):
            for part in range(2):
                first = 32 * quarter + 8 * grp + 4 * part
                turned = pltpu.roll(f_ref[grp, part, rows, :], 4 * (1 - d) + first, 1)
                packed = jnp.where((lane >= first) & (lane < first + 4), turned, packed)
    out_ref[...] = packed.astype(BF16)


def unpack_edge(in_ref, wide_ref, turned_ref):
    lane = iota((64, 128), 1)
    packed = in_ref[...].astype(F32)
    wide_ref[0:8, :] = jnp.zeros((8, 128), F32)
    wide_ref[256:264, :] = jnp.zeros((8, 128), F32)
    for quarter in range(4):
        turned = pltpu.roll(packed, 128 - 32 * quarter, 1) if quarter else packed
        wide_ref[4 + 64 * quarter : 68 + 64 * quarter, :] = jnp.where(lane < 32, turned, 0.0)
    wide = wide_ref[0:264, :]
    for n in range(12):
        turned_ref[n] = pltpu.roll(wide, (8 * (n - 3)) % 128, 1) if n != 3 else wide


def top_edge(d, top_ref, g_ref):
    lane = iota((256, 128), 1)
    other = pl.ds(pl.multiple_of((1 - d) * 128, 128), 128)
    for fr in range(2):
        for s in range(2):
            re = pltpu.roll(top_ref[fr, 2 * s, :, other].astype(F32), 4 * d, 1)
            im = pltpu.roll(top_ref[fr, 2 * s + 1, :, other].astype(F32), 4 + 4 * d, 1)
            g_ref[2 * fr + s, 4:260, :] = jnp.where(lane < 4, re, jnp.where(lane < 8, im, 0.0))


def edge_columns(g_ref, grp, rows):
    edge = g_ref[grp, pl.ds(rows[0], rows[1]), :]
    for a in range(1, 9):
        edge = edge + pltpu.roll(g_ref[grp, pl.ds(rows[0] + a, rows[1]), :], 8 * a, 1)
    return edge.astype(BF16)


def convolve(f_ref, w_ref, o_ref, fr, rows, g_ref=None):
    fields = []
    for grp in (2 * fr, 2 * fr + 1):
        pieces = [
            f_ref[grp, part, pl.ds(rows[0] + a, rows[1]), :].astype(BF16)
            for a in range(9)
            for part in range(2)
        ]
        if g_ref is not None:
            pieces.append(edge_columns(g_ref, grp, rows))
        fields.append(jnp.concatenate(pieces, axis=1))
    left = jnp.concatenate(fields, axis=0)
    depth = slice(0, left.shape[1])
    value = jnp.dot(left, w_ref[fr, 0, depth, :], preferred_element_type=F32) + jnp.dot(
        left, w_ref[fr, 1, depth, :], preferred_element_type=F32
    )
    for s in range(2):
        first = fr * 512 + s * 256 + rows[0]
        o_ref[first : first + rows[1], :] = value[s * rows[1] : (s + 1) * rows[1]]


def add_edge(turned_ref, w_ref, o_ref, rows):
    lane = iota((rows[1], 128), 1)
    for fr in range(2):
        fields = []
        for grp in (2 * fr, 2 * fr + 1):
            edge = jnp.zeros((rows[1], 128), F32)
            for a in range(9):
                here = (lane >= 8 * a) & (lane < 8 * a + 8)
                edge = jnp.where(here, turned_ref[a - grp + 3, pl.ds(rows[0] + a, rows[1]), :], edge)
            fields.append(edge.astype(BF16))
        left = jnp.concatenate(fields, axis=0)
        depth = slice(2304, 2432)
        value = jnp.dot(left, w_ref[fr, 0, depth, :], preferred_element_type=F32) + jnp.dot(
            left, w_ref[fr, 1, depth, :], preferred_element_type=F32
        )
        for s in range(2):
            first = fr * 512 + s * 256 + rows[0]
            o_ref[first : first + rows[1], :] += value[s * rows[1] : (s + 1) * rows[1]]


def cos_sin(angle):
    turns = jnp.round(angle * 0.6366197723675814)
    y = ((angle - turns * 1.5703125) - turns * 4.837512969970703e-4) - turns * 7.549789948768648e-8
    z = y * y
    sine = y + y * z * (-1.6666654611e-1 + z * (8.3321608736e-3 + z * -1.9515295891e-4))
    cosine = (1.0 - 0.5 * z) + z * z * (
        4.166664568298827e-2 + z * (-1.388731625493765e-3 + z * 2.443315711809948e-5)
    )
    quarter = turns.astype(jnp.int32)
    odd = (quarter & 1) == 1
    out_sine = jnp.where(odd, cosine, sine)
    out_cosine = jnp.where(odd, sine, cosine)
    return (
        jnp.where(((quarter + 1) & 2) == 2, -out_cosine, out_cosine),
        jnp.where((quarter & 2) == 2, -out_sine, out_sine),
    )


def cut_screen(slow_ref, off_x, off_y, sides, wide_ref, outs):
    value = slow_ref[...]
    high = value.astype(BF16)
    rest = value - high.astype(F32)
    middle = rest.astype(BF16)
    low = (rest - middle.astype(F32)).astype(BF16)
    lane = iota((384, 256), 1)
    column = jnp.where(lane < 128, lane + 128 * sides[0], lane - 128 + 128 * sides[1]) + off_y
    pick = jnp.where(iota((384, 256), 0) == column, 1.0, 0.0).astype(BF16)
    high, middle, low = (
        jnp.dot(part, pick, preferred_element_type=F32) for part in (high, middle, low)
    )
    moved = high + (middle + low)
    wide_ref[0] = moved[:, 0:128]
    wide_ref[1] = moved[:, 128:256]
    for side in range(2):
        outs[side][...] = wide_ref[side, pl.ds(off_x, 256), :]


def apply_phase(o_ref, screen_ref, weights, f_ref, rows, size):
    for fr in range(2):

        @pl.loop(0, rows[1] // size)
        def _(blk):
            row0 = pl.multiple_of(rows[0] + blk * size, 8)
            angle = (3.0 * weights[fr]) * screen_ref[pl.ds(row0, size), :]
            cosine, sine = cos_sin(angle)
            for s in range(2):
                grp = fr * 2 + s
                here = pl.ds(pl.multiple_of(grp * 256 + row0, 8), size)
                re = o_ref[here, 0:128]
                im = o_ref[here, 128:256]
                f_ref[grp, 0, pl.ds(row0 + 4, size), :] = re * cosine - im * sine
                f_ref[grp, 1, pl.ds(row0 + 4, size), :] = re * sine + im * cosine


def flip_source(f_ref, rev_ref, tiles):
    index = 7 - iota((8, 128), 0)
    for fr in range(2):
        for part in range(2):
            for t in tiles:
                rev_ref[fr, part, 8 * (32 - t) : 8 * (32 - t) + 8, :] = jnp.take_along_axis(
                    f_ref[fr * 2, part, 8 * t : 8 * t + 8, :], index, axis=0
                )


def image_piece(f_ref, rev_ref, img_ref, xx, half):
    @pl.loop(0, NZ // 2)
    def _(z):
        blk = (z + half * 4) * NXX + xx
        row0 = pl.multiple_of(blk * 8, 8)
        rev0 = pl.multiple_of(248 - blk * 8, 8)
        for j in range(8):
            s_rows = pl.ds(rev0 + (7 - j), 8)
            r_rows = pl.ds(row0 + j, 8)
            value = jnp.zeros((8, 128), F32)
            for fr in range(2):
                for part in range(2):
                    value = value + rev_ref[fr, part, s_rows, :] * f_ref[fr * 2 + 1, part, r_rows, :]
            to = pl.multiple_of(half * 128 + (j // 4) * 64 + z * 16 + (j % 2) * 8, 8)
            img_ref[(j // 2) % 2, xx, pl.ds(to, 8), :] = value


def kernel(
    total,
    offsets_ref, taps_ref, slow_hbm, top_hbm, out_ref,
    slow_ref, top_ref, f_ref, last_ref, g_ref, w_ref, edge_ref, o_ref, rev_ref, pad_ref, wide_ref, cut_ref,
    taps_all, screens, screen_tx, turned_ref, edge_tx, edge_rx, img, rx1, tx2, rx2, acc, tx3, rx3, own_part,
    local_sem, s0_send, s0_recv, s1_send, s1_recv, s2_send, s2_recv, s3_send, s3_recv,
):
    d = lax.axis_index("depth")
    f = lax.axis_index("freq")
    core, yhi, xx, z = f % 2, (f // 2) % 2, (f // 4) % NXX, f // 16

    load_top = pltpu.make_async_copy(top_hbm, top_ref, local_sem.at[0])
    load_slow = pltpu.make_async_copy(slow_hbm, slow_ref, local_sem.at[1])

    def device(depth=d, zc=z, xc=xx, yc=yhi, cc=core):
        return (depth, ((zc * NXX + xc) * 2 + yc) * 2 + cc)

    xs, ys = [(xx + off) % NXX for off in range(NXX)], [yhi, 1 - yhi]
    z_peers = [device(zc=(z + off) % NZ) for off in range(1, NZ)]
    core_peer = device(cc=1 - core)
    depth_peer = device(depth=1 - d)
    plane = [
        device(depth=(d + rel) % 2, xc=xs[xo], yc=ys[yo])
        for rel in range(2) for xo in range(NXX) for yo in range(2)
    ][1:]
    everyone = [core_peer] + plane + z_peers
    barrier = pltpu.get_barrier_semaphore()
    for peer in everyone:
        pl.semaphore_signal(barrier, inc=1, device_id=peer, device_id_type=MESH)
    load_slow.start()
    load_top.start()

    def remote(src, dst, send, recv, peer):
        return pltpu.make_async_remote_copy(
            src_ref=src, dst_ref=dst, send_sem=send, recv_sem=recv,
            device_id=peer, device_id_type=MESH,
        )

    swap_taps = remote(taps_all.at[d], taps_all.at[d], s0_send.at[0], s0_recv.at[0], depth_peer)
    swap_screen = remote(screen_tx, screens.at[d], s0_send.at[1], s0_recv.at[1], depth_peer)
    swap_edge = remote(edge_tx, edge_rx, s0_send.at[2], s0_recv.at[2], depth_peer)
    weights = [(2 * f + fr + 1).astype(F32) / total for fr in range(2)]

    def stage1_copy(k, off, part):
        rows = pl.ds(part[0] * 128, part[1] * 128)
        return remote(
            img.at[k, 1 - core, xs[off], rows], rx1.at[k, off, rows],
            s1_send.at[k, part[0], off], s1_recv.at[k, part[0], off], core_peer,
        )

    def stage2_copy(k, xo, yo, part):
        at = ((d + k) % 2) * 8 + xo * 2 + yo
        rows = pl.ds(part[0] * 64, part[1] * 64)
        return remote(
            tx2.at[k, xo * 2 + yo, rows], rx2.at[k, at, rows],
            s2_send.at[k, part[0], xo * 2 + yo], s2_recv.at[k, part[0]],
            device(depth=k, xc=xs[xo], yc=ys[yo]),
        )

    def stage2_get(k, part):
        here = rx2.at[k, pl.ds(1, 15), pl.ds(part[0] * 64, part[1] * 64)]
        return remote(here, here, s2_send.at[k, part[0], 0], s2_recv.at[k, part[0]], depth_peer)

    def stage3_copy(k, to):
        off = (to - z + NZ) % NZ
        return remote(
            tx3.at[k, to], rx3.at[k, off], s3_send.at[k, to], s3_recv.at[k], device(zc=to)
        )

    def stage3_get(k):
        here = rx3.at[k, pl.ds(1, 7)]
        return remote(here, here, s3_send.at[k, 0], s3_recv.at[k], depth_peer)

    def make_image(k, fields, part):
        halves = range(part[0], part[0] + part[1])
        for half in halves:
            flip_source(fields, rev_ref, (range(17), range(17, 33))[half])
        for off in X_ORDER:
            for half in halves:
                image_piece(fields, rev_ref, img.at[k], xs[off], half)
            stage1_copy(k, off, part).start()

    def after_core(k, part):
        for off in X_ORDER:
            stage1_copy(k, off, part).wait_recv()
            for yo in (1, 0):
                for half in range(part[0], part[0] + part[1]):
                    rows = pl.ds(pl.multiple_of(half * 128 + ys[yo] * 64, 64), 64)
                    value = img[k, core, xs[off], rows, :] + rx1[k, off, rows, :]
                    if off == 0 and yo == 0:
                        acc[k, half * 64 : half * 64 + 64, :] = value
                    tx2[k, off * 2 + yo, half * 64 : half * 64 + 64, :] = value.astype(BF16)
                if off or yo:
                    stage2_copy(k, off, yo, part).start()

        @pl.when(d != k)
        def _():
            stage2_copy(k, 0, 0, part).start()

    def after_plane(k, part):
        @pl.when(d == k)
        def _():
            stage2_get(k, part).wait_recv()
            for to in range(4 * part[0], 4 * part[0] + 4 * part[1]):
                rows = pl.ds(to * 16, 16)
                near = acc[k, rows, :]
                for at in range(1, 8):
                    near = near + rx2[k, at, rows, :].astype(F32)
                far = rx2[k, 8, rows, :].astype(F32)
                for at in range(9, 16):
                    far = far + rx2[k, at, rows, :].astype(F32)
                value = jnp.concatenate([near, far], axis=0)
                tx3[k, to] = value.astype(BF16)

                @pl.when(z != to)
                def _():
                    stage3_copy(k, to).start()

                @pl.when(z == to)
                def _():
                    own_part[k] = value

    def after_z(k):
        @pl.when(d == k)
        def _():
            stage3_get(k).wait_recv()
            value = own_part[k]
            for off in range(1, NZ):
                value = value + rx3[k, off].astype(F32)
            for half in range(2):
                lanes = k * 128 if half == 0 else (1 - k) * 128
                for low in range(2):
                    rows = slice(half * 16 + low * 8, half * 16 + low * 8 + 8)
                    out_ref[:, pl.ds(low * 256 + lanes, 128)] = value[rows]

    arrange_taps(taps_ref, pad_ref, taps_all.at[d])
    pl.semaphore_wait(barrier, len(everyone))
    swap_taps.start()
    for ref in (f_ref, last_ref):
        ref[:, :, 0:8, :] = jnp.zeros((4, 2, 8, 128), F32)
        ref[:, :, 256:264, :] = jnp.zeros((4, 2, 8, 128), F32)
    g_ref[:, 0:8, :] = jnp.zeros((4, 8, 128), F32)
    g_ref[:, 256:264, :] = jnp.zeros((4, 8, 128), F32)
    off_x, off_y = offsets_ref[0, 0], offsets_ref[0, 1]
    load_slow.wait()
    cut_screen(slow_ref, off_x, off_y, (1 - d, d), cut_ref, (screen_tx, screens.at[d]))
    swap_screen.start()
    load_top.wait()
    mine = pl.ds(pl.multiple_of(d * 128, 128), 128)
    for fr in range(2):
        for s in range(2):
            for part in range(2):
                f_ref[fr * 2 + s, part, 4:260, :] = top_ref[fr, 2 * s + part, :, mine].astype(F32)
    top_edge(d, top_ref, g_ref)

    swap_taps.wait_recv()
    for fr in range(2):
        build_weights(d, taps_all.at[0, fr], w_ref.at[0, fr], edge_ref.at[0])
    for fr in range(2):
        convolve(f_ref, w_ref.at[0], o_ref, fr, ALL, g_ref)
        build_weights(d, taps_all.at[1, fr], w_ref.at[1, fr], edge_ref.at[1])
    swap_screen.wait_recv()
    apply_phase(o_ref, screens.at[0], weights, f_ref, ALL, 64)
    pack_edge(d, f_ref, edge_tx)
    swap_edge.start()
    make_image(0, f_ref, PARTS[0][0])
    for fr in range(2):
        convolve(f_ref, w_ref.at[1], o_ref, fr, UPPER)
    after_core(0, PARTS[0][0])
    swap_edge.wait_recv()
    unpack_edge(edge_rx, wide_ref, turned_ref)
    add_edge(turned_ref, w_ref.at[1], o_ref, UPPER)
    apply_phase(o_ref, screens.at[1], weights, last_ref, UPPER, 48)
    make_image(1, last_ref, PARTS[1][0])
    for fr in range(2):
        convolve(f_ref, w_ref.at[1], o_ref, fr, LOWER)
    add_edge(turned_ref, w_ref.at[1], o_ref, LOWER)
    apply_phase(o_ref, screens.at[1], weights, last_ref, LOWER, 56)
    make_image(1, last_ref, PARTS[1][1])
    after_core(1, PARTS[1][0])
    after_core(1, PARTS[1][1])
    def sent(k):
        for part in PARTS[k]:
            for off in range(NXX):
                stage1_copy(k, off, part).wait_send()
                for yo in range(2):
                    if off or yo:
                        stage2_copy(k, off, yo, part).wait_send()

        @pl.when(d != k)
        def _():
            for part in PARTS[k]:
                stage2_copy(k, 0, 0, part).wait_send()

    def z_sent(k):
        @pl.when(d == k)
        def _():
            for to in range(NZ):

                @pl.when(z != to)
                def _():
                    stage3_copy(k, to).wait_send()

    for part in PARTS[0]:
        after_plane(0, part)
    sent(0)
    swap_taps.wait_send()
    swap_screen.wait_send()
    swap_edge.wait_send()
    after_z(0)
    for part in PARTS[1]:
        after_plane(1, part)
    sent(1)
    z_sent(0)
    after_z(1)
    z_sent(1)


def migrate(total, offsets, taps, slowness, top):
    dma = pltpu.SemaphoreType.DMA
    vmem = pl.BlockSpec(memory_space=pltpu.VMEM)
    hbm = pl.BlockSpec(memory_space=pl.ANY)
    return pl.pallas_call(
        functools.partial(kernel, total),
        out_shape=pltpu.VMEM((8, 512), F32),
        in_specs=[pl.BlockSpec(memory_space=pltpu.SMEM), vmem, hbm, hbm],
        out_specs=vmem,
        scratch_shapes=[
            pltpu.VMEM((384, 384), F32),
            pltpu.VMEM((2, 4, 256, 256), BF16),
            pltpu.VMEM((4, 2, 264, 128), F32),
            pltpu.VMEM((4, 2, 264, 128), F32),
            pltpu.VMEM((4, 264, 128), F32),
            pltpu.VMEM((2, 2, 2, 2432, 256), BF16),
            pltpu.VMEM((2, 128, 256), F32),
            pltpu.VMEM((1024, 256), F32),
            pltpu.VMEM((2, 2, 264, 128), F32),
            pltpu.VMEM((8, 128), F32),
            pltpu.VMEM((384, 128), F32),
            pltpu.VMEM((2, 384, 128), F32),
            pltpu.VMEM((2, 2, 2, 16, 128), F32),
            pltpu.VMEM((2, 256, 128), F32),
            pltpu.VMEM((256, 128), F32),
            pltpu.VMEM((12, 264, 128), F32),
            pltpu.VMEM((64, 128), BF16),
            pltpu.VMEM((64, 128), BF16),
            pltpu.VMEM((2, 2, NXX, 256, 128), F32),
            pltpu.VMEM((2, NXX, 256, 128), F32),
            pltpu.VMEM((2, 8, 128, 128), BF16),
            pltpu.VMEM((2, 16, 128, 128), BF16),
            pltpu.VMEM((2, 128, 128), F32),
            pltpu.VMEM((2, 8, 32, 128), BF16),
            pltpu.VMEM((2, 8, 32, 128), BF16),
            pltpu.VMEM((2, 32, 128), F32),
            dma((2,)), dma((3,)), dma((3,)), dma((2, 2, 4)), dma((2, 2, 4)), dma((2, 2, 8)), dma((2, 2)),
            dma((2, 8)), dma((2,)),
        ],
        compiler_params=pltpu.CompilerParams(
            collective_id=0, has_side_effects=True, vmem_limit_bytes=56 * 2**20
        ),
    )(offsets, taps, slowness, top)


def local(total, top_fields, slowness, kernels, offsets):
    out = migrate(float(total), offsets, kernels[0], slowness[0], top_fields[0])
    return out[None, None] * float(total) ** -0.5


def solution(mesh):
    return jax.shard_map(
        functools.partial(local, 256),
        mesh=mesh,
        in_specs=(
            P(None, "freq", None, None, None),
            P("depth", None, None),
            P("depth", "freq", None, None),
            P(),
        ),
        out_specs=P("depth", None, None, "freq"),
        check_vma=False,
    )
```

```python
import functools

import jax
import jax.numpy as jnp
from jax import lax
from jax.experimental import pallas as pl
from jax.experimental.pallas import tpu as pltpu
from jax.sharding import PartitionSpec as P

F32, BF16 = jnp.float32, jnp.bfloat16
MESH = pl.DeviceIdType.MESH

NZ, NXX = 8, 4
X_ORDER = (2, 1, 3, 0)
ALL, UPPER, LOWER = (0, 256), (0, 144), (144, 112)
PARTS = (((0, 2),), ((0, 1), (1, 1)))


def iota(shape, dim):
    return lax.broadcasted_iota(jnp.int32, shape, dim)


def split_store(w_ref, rows, cols, value):
    high = value.astype(BF16)
    w_ref[0, rows, cols] = high
    w_ref[1, rows, cols] = (value - high.astype(F32)).astype(BF16)


def arrange_taps(taps_ref, pad_ref, out_ref):
    lane, row = iota((8, 128), 1), iota((8, 128), 0)
    used = (lane < 5) | (lane >= 124)
    place = jnp.where(lane < 5, 4 - lane, 132 - lane)
    pad_ref[...] = jnp.zeros_like(pad_ref)
    for fr in range(2):
        for part in range(2):
            pad_ref[2 * fr + part : 2 * fr + part + 1, 0:81] = taps_ref[fr, part : part + 1, :]
    for fr in range(2):
        for part in range(2):
            line = jnp.broadcast_to(pad_ref[2 * fr + part : 2 * fr + part + 1, :], (8, 128))
            for half in range(2):
                index = jnp.where(used, jnp.minimum(9 * (row + 8 * half), 72) + place, 127)
                out_ref[fr, part, 8 * half : 8 * half + 8, :] = jnp.take_along_axis(line, index, axis=1)


def build_weights(d, taps_ref, w_ref, edge_ref):
    row, col = iota((128, 128), 0), iota((128, 128), 1)
    near = jnp.abs(col - row) <= 4
    row8, col8 = iota((8, 128), 0), iota((8, 128), 1)
    low = row8 < 4
    top_mask = col8 - row8 >= 124
    end_mask = col8 - (row8 + 120) <= -124
    edge_ref[72:128, :] = jnp.zeros((56, 256), F32)
    for a in range(9):
        circ = []
        for part in range(2):
            first = jnp.broadcast_to(taps_ref[part, a : a + 1, :], (128, 128))
            circ.append(pltpu.roll(first, 0, 1, stride=1, stride_axis=0))
        d_r, d_i = (jnp.where(near, m, 0.0) for m in circ)
        base = a * 256
        split_store(w_ref, pl.ds(base, 128), pl.ds(0, 128), d_r)
        split_store(w_ref, pl.ds(base, 128), pl.ds(128, 128), d_i)
        split_store(w_ref, pl.ds(base + 128, 128), pl.ds(0, 128), -d_i)
        split_store(w_ref, pl.ds(base + 128, 128), pl.ds(128, 128), d_r)
        t_r, t_i = (jnp.where(top_mask, m[0:8], 0.0) for m in circ)
        e_r, e_i = (jnp.where(end_mask, m[120:128], 0.0) for m in circ)
        rows = pl.ds(a * 8, 8)
        edge_ref[rows, 0:128] = jnp.where(
            d == 0,
            jnp.where(low, t_r, -pltpu.roll(t_i, 4, 0)),
            jnp.where(low, pltpu.roll(e_r, 4, 0), -e_i),
        )
        edge_ref[rows, 128:256] = jnp.where(
            d == 0,
            jnp.where(low, t_i, pltpu.roll(t_r, 4, 0)),
            jnp.where(low, pltpu.roll(e_i, 4, 0), e_r),
        )
    split_store(w_ref, pl.ds(2304, 128), pl.ds(0, 256), edge_ref[...])


def pack_edge(d, f_ref, out_ref):
    lane = iota((64, 128), 1)
    packed = jnp.zeros((64, 128), F32)
    for quarter in range(4):
        rows = slice(4 + 64 * quarter, 68 + 64 * quarter)
        for grp in range(4):
            for part in range(2):
                first = 32 * quarter + 8 * grp + 4 * part
                turned = pltpu.roll(f_ref[grp, part, rows, :], 4 * (1 - d) + first, 1)
                packed = jnp.where((lane >= first) & (lane < first + 4), turned, packed)
    out_ref[...] = packed.astype(BF16)


def unpack_edge(in_ref, wide_ref, turned_ref):
    lane = iota((64, 128), 1)
    packed = in_ref[...].astype(F32)
    wide_ref[0:8, :] = jnp.zeros((8, 128), F32)
    wide_ref[256:264, :] = jnp.zeros((8, 128), F32)
    for quarter in range(4):
        turned = pltpu.roll(packed, 128 - 32 * quarter, 1) if quarter else packed
        wide_ref[4 + 64 * quarter : 68 + 64 * quarter, :] = jnp.where(lane < 32, turned, 0.0)
    wide = wide_ref[0:264, :]
    for n in range(12):
        turned_ref[n] = pltpu.roll(wide, (8 * (n - 3)) % 128, 1) if n != 3 else wide


def top_edge(d, top_ref, g_ref):
    lane = iota((256, 128), 1)
    other = pl.ds(pl.multiple_of((1 - d) * 128, 128), 128)
    for fr in range(2):
        for s in range(2):
            re = pltpu.roll(top_ref[fr, 2 * s, :, other].astype(F32), 4 * d, 1)
            im = pltpu.roll(top_ref[fr, 2 * s + 1, :, other].astype(F32), 4 + 4 * d, 1)
            g_ref[2 * fr + s, 4:260, :] = jnp.where(lane < 4, re, jnp.where(lane < 8, im, 0.0))


def edge_columns(g_ref, grp, rows):
    edge = g_ref[grp, pl.ds(rows[0], rows[1]), :]
    for a in range(1, 9):
        edge = edge + pltpu.roll(g_ref[grp, pl.ds(rows[0] + a, rows[1]), :], 8 * a, 1)
    return edge.astype(BF16)


def convolve(f_ref, w_ref, o_ref, fr, rows, g_ref=None):
    fields = []
    for grp in (2 * fr, 2 * fr + 1):
        pieces = [
            f_ref[grp, part, pl.ds(rows[0] + a, rows[1]), :].astype(BF16)
            for a in range(9)
            for part in range(2)
        ]
        if g_ref is not None:
            pieces.append(edge_columns(g_ref, grp, rows))
        fields.append(jnp.concatenate(pieces, axis=1))
    left = jnp.concatenate(fields, axis=0)
    depth = slice(0, left.shape[1])
    value = jnp.dot(left, w_ref[fr, 0, depth, :], preferred_element_type=F32) + jnp.dot(
        left, w_ref[fr, 1, depth, :], preferred_element_type=F32
    )
    for s in range(2):
        first = fr * 512 + s * 256 + rows[0]
        o_ref[first : first + rows[1], :] = value[s * rows[1] : (s + 1) * rows[1]]


def add_edge(turned_ref, w_ref, o_ref, rows):
    lane = iota((rows[1], 128), 1)
    for fr in range(2):
        fields = []
        for grp in (2 * fr, 2 * fr + 1):
            edge = jnp.zeros((rows[1], 128), F32)
            for a in range(9):
                here = (lane >= 8 * a) & (lane < 8 * a + 8)
                edge = jnp.where(here, turned_ref[a - grp + 3, pl.ds(rows[0] + a, rows[1]), :], edge)
            fields.append(edge.astype(BF16))
        left = jnp.concatenate(fields, axis=0)
        depth = slice(2304, 2432)
        value = jnp.dot(left, w_ref[fr, 0, depth, :], preferred_element_type=F32) + jnp.dot(
            left, w_ref[fr, 1, depth, :], preferred_element_type=F32
        )
        for s in range(2):
            first = fr * 512 + s * 256 + rows[0]
            o_ref[first : first + rows[1], :] += value[s * rows[1] : (s + 1) * rows[1]]


def cos_sin(angle):
    turns = jnp.round(angle * 0.6366197723675814)
    y = ((angle - turns * 1.5703125) - turns * 4.837512969970703e-4) - turns * 7.549789948768648e-8
    z = y * y
    sine = y + y * z * (-1.6666654611e-1 + z * (8.3321608736e-3 + z * -1.9515295891e-4))
    cosine = (1.0 - 0.5 * z) + z * z * (
        4.166664568298827e-2 + z * (-1.388731625493765e-3 + z * 2.443315711809948e-5)
    )
    quarter = turns.astype(jnp.int32)
    odd = (quarter & 1) == 1
    out_sine = jnp.where(odd, cosine, sine)
    out_cosine = jnp.where(odd, sine, cosine)
    return (
        jnp.where(((quarter + 1) & 2) == 2, -out_cosine, out_cosine),
        jnp.where((quarter & 2) == 2, -out_sine, out_sine),
    )


def cut_screen(slow_ref, off_x, off_y, sides, wide_ref, outs):
    value = slow_ref[...]
    high = value.astype(BF16)
    rest = value - high.astype(F32)
    middle = rest.astype(BF16)
    low = (rest - middle.astype(F32)).astype(BF16)
    lane = iota((384, 256), 1)
    column = jnp.where(lane < 128, lane + 128 * sides[0], lane - 128 + 128 * sides[1]) + off_y
    pick = jnp.where(iota((384, 256), 0) == column, 1.0, 0.0).astype(BF16)
    high, middle, low = (
        jnp.dot(part, pick, preferred_element_type=F32) for part in (high, middle, low)
    )
    moved = high + (middle + low)
    wide_ref[0] = moved[:, 0:128]
    wide_ref[1] = moved[:, 128:256]
    for side in range(2):
        outs[side][...] = wide_ref[side, pl.ds(off_x, 256), :]


def apply_phase(o_ref, screen_ref, weights, f_ref, rows, size):
    for fr in range(2):

        @pl.loop(0, rows[1] // size)
        def _(blk):
            row0 = pl.multiple_of(rows[0] + blk * size, 8)
            angle = (3.0 * weights[fr]) * screen_ref[pl.ds(row0, size), :]
            cosine, sine = cos_sin(angle)
            for s in range(2):
                grp = fr * 2 + s
                here = pl.ds(pl.multiple_of(grp * 256 + row0, 8), size)
                re = o_ref[here, 0:128]
                im = o_ref[here, 128:256]
                f_ref[grp, 0, pl.ds(row0 + 4, size), :] = re * cosine - im * sine
                f_ref[grp, 1, pl.ds(row0 + 4, size), :] = re * sine + im * cosine


def flip_source(f_ref, rev_ref, tiles):
    index = 7 - iota((8, 128), 0)
    for fr in range(2):
        for part in range(2):
            for t in tiles:
                rev_ref[fr, part, 8 * (32 - t) : 8 * (32 - t) + 8, :] = jnp.take_along_axis(
                    f_ref[fr * 2, part, 8 * t : 8 * t + 8, :], index, axis=0
                )


def image_piece(f_ref, rev_ref, img_ref, xx, half):
    @pl.loop(0, NZ // 2)
    def _(z):
        blk = (z + half * 4) * NXX + xx
        row0 = pl.multiple_of(blk * 8, 8)
        rev0 = pl.multiple_of(248 - blk * 8, 8)
        for j in range(8):
            s_rows = pl.ds(rev0 + (7 - j), 8)
            r_rows = pl.ds(row0 + j, 8)
            value = jnp.zeros((8, 128), F32)
            for fr in range(2):
                for part in range(2):
                    value = value + rev_ref[fr, part, s_rows, :] * f_ref[fr * 2 + 1, part, r_rows, :]
            to = pl.multiple_of(half * 128 + (j // 4) * 64 + z * 16 + (j % 2) * 8, 8)
            img_ref[(j // 2) % 2, xx, pl.ds(to, 8), :] = value


def kernel(
    total,
    offsets_ref, taps_ref, slow_hbm, top_hbm, out_ref,
    slow_ref, top_ref, f_ref, last_ref, g_ref, w_ref, edge_ref, o_ref, rev_ref, pad_ref, wide_ref, cut_ref,
    taps_all, screens, screen_tx, turned_ref, edge_tx, edge_rx, img, rx1, tx2, rx2, acc, tx3, rx3, own_part,
    local_sem, s0_send, s0_recv, s1_send, s1_recv, s2_send, s2_recv, s3_send, s3_recv,
):
    d = lax.axis_index("depth")
    f = lax.axis_index("freq")
    core, yhi, xx, z = f % 2, (f // 2) % 2, (f // 4) % NXX, f // 16

    load_top = pltpu.make_async_copy(top_hbm, top_ref, local_sem.at[0])
    load_slow = pltpu.make_async_copy(slow_hbm, slow_ref, local_sem.at[1])

    def device(depth=d, zc=z, xc=xx, yc=yhi, cc=core):
        return (depth, ((zc * NXX + xc) * 2 + yc) * 2 + cc)

    xs, ys = [(xx + off) % NXX for off in range(NXX)], [yhi, 1 - yhi]
    z_peers = [device(zc=(z + off) % NZ) for off in range(1, NZ)]
    core_peer = device(cc=1 - core)
    depth_peer = device(depth=1 - d)
    plane = [
        device(depth=(d + rel) % 2, xc=xs[xo], yc=ys[yo])
        for rel in range(2) for xo in range(NXX) for yo in range(2)
    ][1:]
    everyone = [core_peer] + plane + z_peers
    barrier = pltpu.get_barrier_semaphore()
    for peer in everyone:
        pl.semaphore_signal(barrier, inc=1, device_id=peer, device_id_type=MESH)
    load_slow.start()
    load_top.start()

    def remote(src, dst, send, recv, peer):
        return pltpu.make_async_remote_copy(
            src_ref=src, dst_ref=dst, send_sem=send, recv_sem=recv,
            device_id=peer, device_id_type=MESH,
        )

    swap_taps = remote(taps_all.at[d], taps_all.at[d], s0_send.at[0], s0_recv.at[0], depth_peer)
    swap_screen = remote(screen_tx, screens.at[d], s0_send.at[1], s0_recv.at[1], depth_peer)
    swap_edge = remote(edge_tx, edge_rx, s0_send.at[2], s0_recv.at[2], depth_peer)
    weights = [(2 * f + fr + 1).astype(F32) / total for fr in range(2)]

    def stage1_copy(k, off, part):
        rows = pl.ds(part[0] * 128, part[1] * 128)
        return remote(
            img.at[k, 1 - core, xs[off], rows], rx1.at[k, off, rows],
            s1_send.at[k, part[0], off], s1_recv.at[k, part[0], off], core_peer,
        )

    def stage2_copy(k, xo, yo, part):
        at = ((d + k) % 2) * 8 + xo * 2 + yo
        rows = pl.ds(part[0] * 64, part[1] * 64)
        return remote(
            tx2.at[k, xo * 2 + yo, rows], rx2.at[k, at, rows],
            s2_send.at[k, part[0], xo * 2 + yo], s2_recv.at[k, part[0]],
            device(depth=k, xc=xs[xo], yc=ys[yo]),
        )

    def stage2_get(k, part):
        here = rx2.at[k, pl.ds(1, 15), pl.ds(part[0] * 64, part[1] * 64)]
        return remote(here, here, s2_send.at[k, part[0], 0], s2_recv.at[k, part[0]], depth_peer)

    def stage3_copy(k, to):
        off = (to - z + NZ) % NZ
        return remote(
            tx3.at[k, to], rx3.at[k, off], s3_send.at[k, to], s3_recv.at[k], device(zc=to)
        )

    def stage3_get(k):
        here = rx3.at[k, pl.ds(1, 7)]
        return remote(here, here, s3_send.at[k, 0], s3_recv.at[k], depth_peer)

    def make_image(k, fields, part):
        halves = range(part[0], part[0] + part[1])
        for half in halves:
            flip_source(fields, rev_ref, (range(17), range(17, 33))[half])
        for off in X_ORDER:
            for half in halves:
                image_piece(fields, rev_ref, img.at[k], xs[off], half)
            stage1_copy(k, off, part).start()

    def after_core(k, part):
        for off in X_ORDER:
            stage1_copy(k, off, part).wait_recv()
            for yo in (1, 0):
                for half in range(part[0], part[0] + part[1]):
                    rows = pl.ds(pl.multiple_of(half * 128 + ys[yo] * 64, 64), 64)
                    value = img[k, core, xs[off], rows, :] + rx1[k, off, rows, :]
                    if off == 0 and yo == 0:
                        acc[k, half * 64 : half * 64 + 64, :] = value
                    tx2[k, off * 2 + yo, half * 64 : half * 64 + 64, :] = value.astype(BF16)
                if off or yo:
                    stage2_copy(k, off, yo, part).start()

        @pl.when(d != k)
        def _():
            stage2_copy(k, 0, 0, part).start()

    def after_plane(k, part):
        @pl.when(d == k)
        def _():
            stage2_get(k, part).wait_recv()
            count = 4 * part[1]
            for step in range(count):
                to = 4 * part[0] + (z + step) % count
                rows = pl.ds(pl.multiple_of(to * 16, 16), 16)
                near = acc[k, rows, :]
                for at in range(1, 8):
                    near = near + rx2[k, at, rows, :].astype(F32)
                far = rx2[k, 8, rows, :].astype(F32)
                for at in range(9, 16):
                    far = far + rx2[k, at, rows, :].astype(F32)
                value = jnp.concatenate([near, far], axis=0)
                tx3[k, to] = value.astype(BF16)

                @pl.when(z != to)
                def _():
                    stage3_copy(k, to).start()

                @pl.when(z == to)
                def _():
                    own_part[k] = value

    def after_z(k):
        @pl.when(d == k)
        def _():
            stage3_get(k).wait_recv()
            value = own_part[k]
            for off in range(1, NZ):
                value = value + rx3[k, off].astype(F32)
            for half in range(2):
                lanes = k * 128 if half == 0 else (1 - k) * 128
                for low in range(2):
                    rows = slice(half * 16 + low * 8, half * 16 + low * 8 + 8)
                    out_ref[:, pl.ds(low * 256 + lanes, 128)] = value[rows] * total**-0.5

    arrange_taps(taps_ref, pad_ref, taps_all.at[d])
    pl.semaphore_wait(barrier, len(everyone))
    swap_taps.start()
    for ref in (f_ref, last_ref):
        ref[:, :, 0:8, :] = jnp.zeros((4, 2, 8, 128), F32)
        ref[:, :, 256:264, :] = jnp.zeros((4, 2, 8, 128), F32)
    g_ref[:, 0:8, :] = jnp.zeros((4, 8, 128), F32)
    g_ref[:, 256:264, :] = jnp.zeros((4, 8, 128), F32)
    off_x, off_y = offsets_ref[0, 0], offsets_ref[0, 1]
    load_slow.wait()
    cut_screen(slow_ref, off_x, off_y, (1 - d, d), cut_ref, (screen_tx, screens.at[d]))
    swap_screen.start()
    load_top.wait()
    mine = pl.ds(pl.multiple_of(d * 128, 128), 128)
    for fr in range(2):
        for s in range(2):
            for part in range(2):
                f_ref[fr * 2 + s, part, 4:260, :] = top_ref[fr, 2 * s + part, :, mine].astype(F32)
    top_edge(d, top_ref, g_ref)

    swap_taps.wait_recv()
    for fr in range(2):
        build_weights(d, taps_all.at[0, fr], w_ref.at[0, fr], edge_ref.at[0])
    for fr in range(2):
        convolve(f_ref, w_ref.at[0], o_ref, fr, ALL, g_ref)
        build_weights(d, taps_all.at[1, fr], w_ref.at[1, fr], edge_ref.at[1])
    swap_screen.wait_recv()
    apply_phase(o_ref, screens.at[0], weights, f_ref, ALL, 64)
    pack_edge(d, f_ref, edge_tx)
    swap_edge.start()
    make_image(0, f_ref, PARTS[0][0])
    for fr in range(2):
        convolve(f_ref, w_ref.at[1], o_ref, fr, UPPER)
    after_core(0, PARTS[0][0])
    swap_edge.wait_recv()
    unpack_edge(edge_rx, wide_ref, turned_ref)
    add_edge(turned_ref, w_ref.at[1], o_ref, UPPER)
    apply_phase(o_ref, screens.at[1], weights, last_ref, UPPER, 48)
    make_image(1, last_ref, PARTS[1][0])
    for fr in range(2):
        convolve(f_ref, w_ref.at[1], o_ref, fr, LOWER)
    add_edge(turned_ref, w_ref.at[1], o_ref, LOWER)
    apply_phase(o_ref, screens.at[1], weights, last_ref, LOWER, 56)
    make_image(1, last_ref, PARTS[1][1])
    after_core(1, PARTS[1][0])
    after_core(1, PARTS[1][1])
    def sent(k):
        for part in PARTS[k]:
            for off in range(NXX):
                stage1_copy(k, off, part).wait_send()
                for yo in range(2):
                    if off or yo:
                        stage2_copy(k, off, yo, part).wait_send()

        @pl.when(d != k)
        def _():
            for part in PARTS[k]:
                stage2_copy(k, 0, 0, part).wait_send()

    def z_sent(k):
        @pl.when(d == k)
        def _():
            for to in range(NZ):

                @pl.when(z != to)
                def _():
                    stage3_copy(k, to).wait_send()

    for part in PARTS[0]:
        after_plane(0, part)
    sent(0)
    swap_taps.wait_send()
    swap_screen.wait_send()
    swap_edge.wait_send()
    after_z(0)
    for part in PARTS[1]:
        after_plane(1, part)
    sent(1)
    z_sent(0)
    after_z(1)
    z_sent(1)


def migrate(total, offsets, taps, slowness, top):
    dma = pltpu.SemaphoreType.DMA
    vmem = pl.BlockSpec(memory_space=pltpu.VMEM)
    hbm = pl.BlockSpec(memory_space=pl.ANY)
    return pl.pallas_call(
        functools.partial(kernel, total),
        out_shape=pltpu.VMEM((8, 512), F32),
        in_specs=[pl.BlockSpec(memory_space=pltpu.SMEM), vmem, hbm, hbm],
        out_specs=vmem,
        scratch_shapes=[
            pltpu.VMEM((384, 384), F32),
            pltpu.VMEM((2, 4, 256, 256), BF16),
            pltpu.VMEM((4, 2, 264, 128), F32),
            pltpu.VMEM((4, 2, 264, 128), F32),
            pltpu.VMEM((4, 264, 128), F32),
            pltpu.VMEM((2, 2, 2, 2432, 256), BF16),
            pltpu.VMEM((2, 128, 256), F32),
            pltpu.VMEM((1024, 256), F32),
            pltpu.VMEM((2, 2, 264, 128), F32),
            pltpu.VMEM((8, 128), F32),
            pltpu.VMEM((384, 128), F32),
            pltpu.VMEM((2, 384, 128), F32),
            pltpu.VMEM((2, 2, 2, 16, 128), F32),
            pltpu.VMEM((2, 256, 128), F32),
            pltpu.VMEM((256, 128), F32),
            pltpu.VMEM((12, 264, 128), F32),
            pltpu.VMEM((64, 128), BF16),
            pltpu.VMEM((64, 128), BF16),
            pltpu.VMEM((2, 2, NXX, 256, 128), F32),
            pltpu.VMEM((2, NXX, 256, 128), F32),
            pltpu.VMEM((2, 8, 128, 128), BF16),
            pltpu.VMEM((2, 16, 128, 128), BF16),
            pltpu.VMEM((2, 128, 128), F32),
            pltpu.VMEM((2, 8, 32, 128), BF16),
            pltpu.VMEM((2, 8, 32, 128), BF16),
            pltpu.VMEM((2, 32, 128), F32),
            dma((2,)), dma((3,)), dma((3,)), dma((2, 2, 4)), dma((2, 2, 4)), dma((2, 2, 8)), dma((2, 2)),
            dma((2, 8)), dma((2,)),
        ],
        compiler_params=pltpu.CompilerParams(
            collective_id=0, has_side_effects=True, vmem_limit_bytes=56 * 2**20
        ),
    )(offsets, taps, slowness, top)


def local(total, top_fields, slowness, kernels, offsets):
    out = migrate(float(total), offsets, kernels[0], slowness[0], top_fields[0])
    return out[None, None]


def solution(mesh):
    return jax.shard_map(
        functools.partial(local, 256),
        mesh=mesh,
        in_specs=(
            P(None, "freq", None, None, None),
            P("depth", None, None),
            P("depth", "freq", None, None),
            P(),
        ),
        out_specs=P("depth", None, None, "freq"),
        check_vma=False,
    )
```
